32 devices in a mesh: groups: 2 (over x), dp: 16 (over z, y, core).
Axes of the slice: x: 2, y: 2, z: 4, core: 2. Of those that a mesh axis runs over, the one named last changes fastest.
Arguments:
- token_inputs: bfloat16 [64, 128, 2048], P(('groups', 'dp')), parts along dimension 0, may hold values from -6 to 6
- state_in: bfloat16 [64, 128, 1, 256], P(('groups', 'dp')), parts along dimension 0, may hold values from -0.03125 to 0.03125
- state_out: bfloat16 [64, 128, 1, 256], P(('groups', 'dp')), parts along dimension 0, may hold values from -0.375 to 0.375
- log_decay: float32 [64, 128, 32], P(('groups', 'dp')), parts along dimension 0, may hold values from -0.8 to 0
- skip_gain: float32 [32], replicated, may hold values from 0.25 to 2.5
- conv_weight: float32 [4, 2048], replicated, may hold values from -3 to 3
- out_cotangent: bfloat16 [64, 128, 2048], P(('groups', 'dp')), parts along dimension 0, may hold values from -1.5 to 1.5
- queries: bfloat16 [64, 128, 4096], P(('groups', 'dp')), parts along dimension 0, may hold values from -12 to 12
- own_keys: bfloat16 [64, 128, 512], P(('groups', 'dp')), parts along dimension 0, may hold values from -4 to 4
- own_values: bfloat16 [64, 128, 512], P(('groups', 'dp')), parts along dimension 0, may hold values from -6 to 6
- attn_cotangent: bfloat16 [64, 128, 4096], P(('groups', 'dp')), parts along dimension 0, may hold values from -6 to 6
- resp_length: int32 [64], P(('groups', 'dp')), parts along dimension 0, may hold values from 32 to 128
- resp_prefix: int32 [64], P('groups'), parts along dimension 0, may hold values from 0 to 15, as said below
- prefix_state: bfloat16 [32, 32, 64, 256], P(('groups', 'dp')), parts along dimension 0, may hold values from -3 to 3
- prefix_tail: bfloat16 [32, 3, 2048], P(('groups', 'dp')), parts along dimension 0, may hold values from -6 to 6
- prefix_keys: bfloat16 [32, 128, 512], P(('groups', 'dp')), parts along dimension 0, may hold values from -4 to 4
- prefix_values: bfloat16 [32, 128, 512], P(('groups', 'dp')), parts along dimension 0, may hold values from -6 to 6
- prefix_length: int32 [32], P('groups'), parts along dimension 0, may hold values from 32 to 128
Outputs:
- grad_inputs: bfloat16 [64, 128, 2048], P(('groups', 'dp')), parts along dimension 0
- grad_read: bfloat16 [64, 128, 1, 256], P(('groups', 'dp')), parts along dimension 0
- grad_queries: bfloat16 [64, 128, 4096], P(('groups', 'dp')), parts along dimension 0
- grad_state: bfloat16 [32, 32, 64, 256], P(('groups', 'dp')), parts along dimension 0
- grad_tail: float32 [32, 3, 2048], P(('groups', 'dp')), parts along dimension 0
- grad_prefix_keys: float32 [32, 128, 512], P(('groups', 'dp')), parts along dimension 0
- grad_prefix_values: float32 [32, 128, 512], P(('groups', 'dp')), parts along dimension 0
- grad_conv: float32 [8, 2048], P('groups'), parts along dimension 0
The draws below stay inside these ranges and needn't reach their ends.
There are 2 independent parts, one for each index of `groups`. The reference program is written for one: setup_inputs(seed, part) draws one part's arguments, and reference() takes and returns one part's arrays. A program takes and returns all parts, laid end to end along the dimension named above; an argument that names none is the same for every part. Nothing has to cross between parts.
Inputs may be any that keep to these rules, and one draw needn't show every extreme that they name: `resp_prefix`: prefix p is owned by device p; response r lies on device r // 2, and its prefix's owner is that device or one of the 3 devices before it, counted cyclically over the devices of dp.
All inputs are finite; a program needn't handle non-finite values.
Results may differ from the reference program's by a relative error of at most 0.0098.
Values may be sent and summed in bfloat16 or wider, within the bound.
No kernel may reach another device: no remote copies, remote signals or barrier semaphores. Data moves between devices by JAX's collectives and lax.ppermute only.
A program may use at most 128 MiB of HBM per device.

```python
import math
import jax
import jax.numpy as jnp
from jax import lax

HEADS = 32
HEAD_DIM = 64
STATE = 256
BC_GROUPS = 1
CONV = 4
ATT_HEADS = 32
KV_HEADS = 4
ATT_DIM = 128
RESP_DEV = 2
ANSWER_POSITIONS = 128
PREF_LEN = 128
PREF_DEV = 1
SPAN = 4
CHANNELS = 2048
ANSWER_TOTAL = 32
PREFIXES = 16
TOKENS = 4096


def base_keys(key):
    return jnp.clip(jax.random.normal(key, (ANSWER_TOTAL, ANSWER_POSITIONS, KV_HEADS * ATT_DIM), jnp.float32), -4.0, 4.0)


def draw_own_keys(key, part):
    common = base_keys(key)
    return common.astype(jnp.bfloat16)


def draw_queries(key, part):
    key = jax.random.fold_in(key, 5)
    shape = (ANSWER_TOTAL, ANSWER_POSITIONS, ATT_HEADS * ATT_DIM)
    return jnp.clip(jax.random.normal(key, shape, jnp.float32), -4.0, 4.0).astype(jnp.bfloat16)


def draw_log_decay(key, part):
    key = jax.random.fold_in(key, 7)
    derived_seed_parts = jax.random.split(key, 5)
    low_rate, high_rate = (math.log(0.1 / ANSWER_POSITIONS), math.log(0.04))
    probability_level = jnp.exp(jax.random.uniform(derived_seed_parts[0], (HEADS,), jnp.float32, low_rate, high_rate))
    contributor_device = jnp.exp(jax.random.uniform(derived_seed_parts[1], (ANSWER_TOTAL, 1, 1), jnp.float32, math.log(0.5), 0.0))
    approximate_guess = jax.random.uniform(derived_seed_parts[2], (ANSWER_TOTAL, ANSWER_POSITIONS, HEADS), jnp.float32, 0.4, 1.6)
    contiguous_span_size = jax.random.bernoulli(derived_seed_parts[3], 2.0 / ANSWER_POSITIONS, (ANSWER_TOTAL, ANSWER_POSITIONS, 1))
    survival_proportion = jax.random.uniform(derived_seed_parts[4], (ANSWER_TOTAL, ANSWER_POSITIONS, 1), jnp.float32, 0.5, 0.8)
    return -probability_level[None, None, :] * contributor_device * approximate_guess + jnp.where(contiguous_span_size, jnp.log(survival_proportion), 0.0)


def draw_resp_prefix(key, part):
    key = jax.random.fold_in(key, 11)
    first_key, second_key = jax.random.split(key)
    devices = ANSWER_TOTAL // RESP_DEV
    home = jnp.arange(ANSWER_TOTAL, dtype=jnp.int32) // RESP_DEV
    offset = jax.random.randint(first_key, (ANSWER_TOTAL,), 0, SPAN, dtype=jnp.int32)
    slot_index = jax.random.randint(second_key, (ANSWER_TOTAL,), 0, PREF_DEV, dtype=jnp.int32)
    offset = offset.at[0].set(SPAN - 1).at[RESP_DEV].set(1).at[ANSWER_TOTAL - 1].set(0)
    slot_index = slot_index.at[RESP_DEV].set(0).at[ANSWER_TOTAL - 1].set(PREF_DEV - 1)
    owner = jnp.mod(home - offset, devices)
    return (owner * PREF_DEV + slot_index).astype(jnp.int32)


def draw_resp_length(key, part):
    key = jax.random.fold_in(key, 13)
    drawn = jax.random.randint(key, (ANSWER_TOTAL,), max(1, ANSWER_POSITIONS // 4), ANSWER_POSITIONS + 1, dtype=jnp.int32)
    return drawn.at[0].set(ANSWER_POSITIONS)


def draw_prefix_length(key, part):
    key = jax.random.fold_in(key, 17)
    drawn = jax.random.randint(key, (PREFIXES,), max(1, PREF_LEN // 4), PREF_LEN + 1, dtype=jnp.int32)
    return drawn.at[0].set(PREF_LEN)


def block_levels(stream_key, extent, cuts, least, high):
    def one(dim, shards_of):
        steps = jax.random.uniform(jax.random.fold_in(jax.random.fold_in(stream_key, 6), dim), (shards_of,), jnp.float32, least / len(cuts), high / len(cuts))
        return jnp.repeat(jnp.exp(steps), extent[dim] // shards_of).reshape((-1,) + (1,) * (len(extent) - dim - 1))

    level = one(*cuts[0])
    for cut in cuts[1:]:
        level = level * one(*cut)
    return level


def normal_values(own_key, shape, width, most, cuts=(), kind=jnp.bfloat16):
    level = block_levels(own_key, shape, cuts, -0.22, 0.18) if cuts else 1.0
    values = jax.random.normal(own_key, shape, jnp.float32) * width * level
    return jnp.minimum(jnp.maximum(values, -most), most).astype(kind)


def setup_inputs(seed: int = 0, part: int = 0) -> dict:
    arg_keys = jax.random.split(jax.random.key(seed), 19)
    part_splits = jax.random.split(jax.random.fold_in(arg_keys[18], part), 19)
    token_inputs = normal_values(part_splits[0], (ANSWER_TOTAL, ANSWER_POSITIONS, CHANNELS), 1.0, 6.0, ((0, 16),))
    state_in = normal_values(part_splits[1], (ANSWER_TOTAL, ANSWER_POSITIONS, BC_GROUPS, STATE), (STATE * ANSWER_POSITIONS) ** -0.5, 0.03125, ((0, 16),))
    state_out = normal_values(part_splits[2], (ANSWER_TOTAL, ANSWER_POSITIONS, BC_GROUPS, STATE), STATE ** -0.5, 0.375, ((0, 16),))
    log_decay = draw_log_decay(jax.random.fold_in(jax.random.fold_in(arg_keys[18], part), 71), part)
    skip_gain = jnp.clip(jax.random.uniform(arg_keys[4], (HEADS,), jnp.float32, 0.25, 2.5), 0.25, 2.5)
    conv_weight = normal_values(arg_keys[5], (CONV, CHANNELS), CONV ** -0.5, 3.0, (), jnp.float32)
    out_cotangent = normal_values(part_splits[6], (ANSWER_TOTAL, ANSWER_POSITIONS, CHANNELS), 0.25, 1.5, ((0, 16),))
    queries = draw_queries(jax.random.fold_in(jax.random.fold_in(arg_keys[18], part), 71), part)
    own_keys = draw_own_keys(jax.random.fold_in(jax.random.fold_in(arg_keys[18], part), 71), part)
    own_values = normal_values(part_splits[9], (ANSWER_TOTAL, ANSWER_POSITIONS, KV_HEADS * ATT_DIM), 1.0, 6.0, ((0, 16),))
    attn_cotangent = normal_values(part_splits[10], (ANSWER_TOTAL, ANSWER_POSITIONS, ATT_HEADS * ATT_DIM), 1.0, 6.0, ((0, 16),))
    resp_length = draw_resp_length(jax.random.fold_in(jax.random.fold_in(arg_keys[18], part), 71), part)
    resp_prefix = draw_resp_prefix(jax.random.fold_in(jax.random.fold_in(arg_keys[18], part), 71), part)
    prefix_state = normal_values(part_splits[13], (PREFIXES, HEADS, HEAD_DIM, STATE), 0.5, 3.0, ((0, 16),))
    prefix_tail = normal_values(part_splits[14], (PREFIXES, CONV - 1, CHANNELS), 1.0, 6.0, ((0, 16),))
    prefix_keys = normal_values(part_splits[15], (PREFIXES, PREF_LEN, KV_HEADS * ATT_DIM), 1.0, 4.0, ((0, 16),))
    prefix_values = normal_values(part_splits[16], (PREFIXES, PREF_LEN, KV_HEADS * ATT_DIM), 1.0, 6.0, ((0, 16),))
    prefix_length = draw_prefix_length(jax.random.fold_in(jax.random.fold_in(arg_keys[18], part), 71), part)
    return {"token_inputs": token_inputs, "state_in": state_in, "state_out": state_out, "log_decay": log_decay, "skip_gain": skip_gain, "conv_weight": conv_weight, "out_cotangent": out_cotangent, "queries": queries, "own_keys": own_keys, "own_values": own_values, "attn_cotangent": attn_cotangent, "resp_length": resp_length, "resp_prefix": resp_prefix, "prefix_state": prefix_state, "prefix_tail": prefix_tail, "prefix_keys": prefix_keys, "prefix_values": prefix_values, "prefix_length": prefix_length}


HIGHEST = lax.Precision.HIGHEST
NEG_FILL = -1e+30

def mamba_grads(inputs, conv_tail, conv_weight, write_proj, read_proj, log_decay, skip_gain, carry_state, cotangent):
    length = inputs.shape[0]
    conv_taps = conv_weight.shape[0]
    head_count, head_width, state_width = carry_state.shape
    group_count = read_proj.shape[1]
    per_group = head_count // group_count

    def activate(inputs, conv_tail, conv_weight):
        padded = jnp.concatenate([conv_tail, inputs], axis=0)
        mixed = conv_weight[0] * padded[0:length]
        for tap_index in range(1, conv_taps):
            mixed = mixed + conv_weight[tap_index] * padded[tap_index:tap_index + length]
        return mixed * jax.nn.sigmoid(mixed)
    act_flat, act_pull = jax.vjp(activate, inputs, conv_tail, conv_weight)
    activated = act_flat.reshape(length, head_count, head_width)
    decay_sum = jnp.cumsum(log_decay, axis=0)
    read_heads = jnp.repeat(read_proj, per_group, axis=1)
    intersection = jnp.einsum('tgn,sgn->gts', read_proj, write_proj, preferred_element_type=jnp.float32)
    intersection = jnp.repeat(intersection, per_group, axis=0)
    row_index = lax.broadcasted_iota(jnp.int32, (length, length), 0)
    col_index = lax.broadcasted_iota(jnp.int32, (length, length), 1)
    causal = (col_index <= row_index)[None]
    lagged = decay_sum.T[:, :, None] - decay_sum.T[:, None, :]
    decay_weights = jnp.where(causal, jnp.exp(jnp.where(causal, lagged, 0.0)), 0.0)
    weights = decay_weights * intersection
    d_out = cotangent.reshape(length, head_count, head_width)
    d_carried = jnp.exp(decay_sum)[:, :, None] * d_out
    g_state = jnp.einsum('thp,thn->hpn', d_carried, read_heads.astype(jnp.float32), precision=HIGHEST)
    d_read_heads = jnp.einsum('thp,hpn->thn', d_carried, carry_state.astype(jnp.float32), precision=HIGHEST)
    g_read = d_read_heads.reshape(length, group_count, per_group, state_width).sum(axis=2)
    d_weights = jnp.einsum('thp,shp->hts', d_out, activated, precision=HIGHEST)
    d_intersection = (d_weights * decay_weights).reshape(group_count, per_group, length, length).sum(axis=1)
    g_read = g_read + jnp.einsum('gts,sgn->tgn', d_intersection, write_proj.astype(jnp.float32), precision=HIGHEST)
    d_act = jnp.einsum('hts,thp->shp', weights, d_out, precision=HIGHEST) + skip_gain[None, :, None] * d_out
    g_inputs, g_tail, g_conv = act_pull(d_act.reshape(length, head_count * head_width))
    return (g_inputs, g_tail, g_conv, g_read, g_state)

def attention_grads(queries, own_keys, own_values, prefix_keys, prefix_values, prefix_length, cotangent):
    length = queries.shape[0]
    pref_rows = prefix_keys.shape[0]
    scale = 1.0 / math.sqrt(ATT_DIM)
    grouped_q = queries.reshape(length, KV_HEADS, ATT_HEADS // KV_HEADS, ATT_DIM)
    all_keys = jnp.concatenate([prefix_keys, own_keys], axis=0).reshape(pref_rows + length, KV_HEADS, ATT_DIM)
    all_values = jnp.concatenate([prefix_values, own_values], axis=0).reshape(pref_rows + length, KV_HEADS, ATT_DIM)
    scores = jnp.einsum('tkrd,skd->krts', grouped_q, all_keys, preferred_element_type=jnp.float32) * scale
    row_index = lax.broadcasted_iota(jnp.int32, (length, pref_rows + length), 0)
    col_index = lax.broadcasted_iota(jnp.int32, (length, pref_rows + length), 1)
    allowed = jnp.where(col_index < pref_rows, col_index < prefix_length, col_index - pref_rows <= row_index)
    scores = jnp.where(allowed[None, None], scores, NEG_FILL)
    top_score = lax.optimization_barrier(jnp.max(scores, axis=-1, keepdims=True))
    raised = jnp.exp(scores - top_score)
    probs = raised / lax.optimization_barrier(jnp.sum(raised, axis=-1, keepdims=True))
    probs_low = probs.astype(jnp.bfloat16)
    output = jnp.einsum('krts,skd->tkrd', probs_low, all_values, preferred_element_type=jnp.float32)
    d_out = cotangent.reshape(length, KV_HEADS, ATT_HEADS // KV_HEADS, ATT_DIM)
    d_probs = jnp.einsum('tkrd,skd->krts', d_out, all_values, preferred_element_type=jnp.float32)
    delta = jnp.transpose(lax.optimization_barrier(jnp.sum(d_out.astype(jnp.float32) * output, axis=-1)), (1, 2, 0))
    d_scores = (probs * (d_probs - delta[..., None]) * scale).astype(jnp.bfloat16)
    g_query = jnp.einsum('krts,skd->tkrd', d_scores, all_keys, preferred_element_type=jnp.float32)
    g_keys = jnp.einsum('krts,tkrd->skd', d_scores, grouped_q, preferred_element_type=jnp.float32)
    g_values = jnp.einsum('krts,tkrd->skd', probs_low, d_out, preferred_element_type=jnp.float32)
    return (g_query.reshape(length, ATT_HEADS * ATT_DIM), g_keys[0:pref_rows].reshape(pref_rows, KV_HEADS * ATT_DIM), g_values[0:pref_rows].reshape(pref_rows, KV_HEADS * ATT_DIM))

def response_grads(inputs, write_proj, read_proj, log_decay, out_cotangent, queries, own_keys, own_values, attn_cotangent, resp_length, prefix_state, prefix_tail, prefix_keys, prefix_values, prefix_length, conv_weight, skip_gain):
    live_rows = (lax.broadcasted_iota(jnp.int32, (inputs.shape[0], 1), 0) < resp_length).astype(jnp.float32)
    g_inputs, g_tail, g_conv, g_read, g_state = mamba_grads(inputs.astype(jnp.float32), prefix_tail.astype(jnp.float32), conv_weight, write_proj, read_proj, log_decay, skip_gain, prefix_state, out_cotangent.astype(jnp.float32) * live_rows)
    masked_cot = jnp.where(live_rows > 0.5, attn_cotangent, jnp.zeros((), attn_cotangent.dtype))
    g_query, g_keys, g_values = attention_grads(queries, own_keys, own_values, prefix_keys, prefix_values, prefix_length, masked_cot)
    return (g_inputs, g_tail, g_conv, g_read, g_state, g_query, g_keys, g_values)

def reference(token_inputs, state_in, state_out, log_decay, skip_gain, conv_weight, out_cotangent, queries, own_keys, own_values, attn_cotangent, resp_length, resp_prefix, prefix_state, prefix_tail, prefix_keys, prefix_values, prefix_length):

    def one_response(carry, position):
        state_acc, tail_acc, key_acc, value_acc, conv_acc = carry
        which = resp_prefix[position]
        grads = response_grads(token_inputs[position], state_in[position], state_out[position], log_decay[position], out_cotangent[position], queries[position], own_keys[position], own_values[position], attn_cotangent[position], resp_length[position], prefix_state[which], prefix_tail[which], prefix_keys[which], prefix_values[which], prefix_length[which], conv_weight, skip_gain)
        g_inputs, g_tail, g_conv, g_read, g_state, g_query, g_keys, g_values = grads
        carry = (state_acc.at[which].add(g_state), tail_acc.at[which].add(g_tail), key_acc.at[which].add(g_keys), value_acc.at[which].add(g_values), conv_acc + g_conv)
        return (carry, (g_inputs.astype(jnp.bfloat16), g_read.astype(jnp.bfloat16), g_query.astype(jnp.bfloat16)))
    start = (jnp.zeros(prefix_state.shape, jnp.float32), jnp.zeros(prefix_tail.shape, jnp.float32), jnp.zeros(prefix_keys.shape, jnp.float32), jnp.zeros(prefix_values.shape, jnp.float32), jnp.zeros(conv_weight.shape, jnp.float32))
    carry, stacked = lax.scan(one_response, start, jnp.arange(ANSWER_TOTAL, dtype=jnp.int32))
    state_acc, tail_acc, key_acc, value_acc, conv_acc = carry
    grad_conv = conv_acc * (1.0 / math.sqrt(TOKENS))
    return (stacked[0], stacked[1], stacked[2], state_acc.astype(jnp.bfloat16), tail_acc, key_acc, value_acc, grad_conv)
```

```python
import functools
import math

import jax
import jax.numpy as jnp
from jax import lax
from jax.experimental import pallas as pl
from jax.experimental.pallas import tpu as pltpu
from jax.sharding import PartitionSpec as P

ATT_HEADS = 32
KV_HEADS = 4
ATT_DIM = 128
HEADS = 32
HEAD_DIM = 64
SPAN = 4
REPEAT = ATT_HEADS // KV_HEADS
NEG_FILL = -1e30
F32 = jnp.float32
BF16 = jnp.bfloat16

SMEM = pl.BlockSpec(memory_space=pltpu.SMEM)
VMEM = pl.BlockSpec(memory_space=pltpu.VMEM)


def shift(value, by):
    length = lax.axis_size("dp")
    return lax.ppermute(value, "dp", [(i, (i + by) % length) for i in range(length)])


def nt(a, b):
    return lax.dot_general(a, b, (((1,), (1,)), ((), ())), preferred_element_type=F32)


def tn(a, b):
    return lax.dot_general(a, b, (((0,), (0,)), ((), ())), preferred_element_type=F32)


def nn(a, b):
    return lax.dot_general(a, b, (((1,), (0,)), ((), ())), preferred_element_type=F32)


def pack_kernel(keys, values, tail, out, rows8):
    rows = keys.shape[1]
    out[0, 0:rows, :] = keys[0]
    out[1, 0:rows, :] = values[0]
    rows8[...] = jnp.zeros_like(rows8)
    rows8[5:8, :] = tail[0].astype(F32)
    for half in range(2):
        upper = rows8[:, half * 1024 : half * 1024 + 512]
        lower = rows8[:, half * 1024 + 512 : half * 1024 + 1024]
        out[half, rows : rows + 16, :] = jnp.concatenate([upper, lower], axis=0).astype(BF16)


def pack(prefix_keys, prefix_values, prefix_tail):
    rows, width = prefix_keys.shape[1:]
    return pl.pallas_call(
        pack_kernel,
        out_shape=jax.ShapeDtypeStruct((2, rows + 16, width), BF16),
        in_specs=[VMEM] * 3,
        out_specs=VMEM,
        scratch_shapes=[pltpu.VMEM((8, prefix_tail.shape[2]), F32)],
        name="pack_prefix",
    )(prefix_keys, prefix_values, prefix_tail)


def running_sum(log_decay):
    length = log_decay.shape[0]
    row = lax.broadcasted_iota(jnp.int32, (length, length), 0)
    col = lax.broadcasted_iota(jnp.int32, (length, length), 1)
    lower = (col <= row).astype(F32)
    return lax.dot_general(
        lower,
        log_decay,
        (((1,), (0,)), ((), ())),
        precision=lax.Precision.HIGHEST,
        preferred_element_type=F32,
    )


def carry_kernel(resp_length, log_decay, cotangent, read, out):
    length = log_decay.shape[1]
    width = cotangent.shape[2]
    live_to = resp_length[pl.program_id(0)]
    raised = jnp.exp(running_sum(log_decay[0]))
    live = lax.broadcasted_iota(jnp.int32, (length, 2 * HEAD_DIM), 0) < live_to
    first = lax.broadcasted_iota(jnp.int32, (length, 2 * HEAD_DIM), 1) < HEAD_DIM
    for pair in range(width // (2 * HEAD_DIM)):
        lanes = slice(pair * 2 * HEAD_DIM, (pair + 1) * 2 * HEAD_DIM)
        factor = jnp.where(first, raised[:, 2 * pair : 2 * pair + 1], raised[:, 2 * pair + 1 : 2 * pair + 2])
        factor = jnp.where(live, factor, 0.0)
        out[0, :, lanes] = (factor * cotangent[0, :, lanes].astype(F32)).astype(BF16)
    out[0, :, width:] = read[0]


def carry(resp_length, log_decay, out_cotangent, state_out):
    count, length, width = out_cotangent.shape
    heads = log_decay.shape[2]
    states = state_out.shape[2]
    return pl.pallas_call(
        carry_kernel,
        grid=(count,),
        out_shape=jax.ShapeDtypeStruct((count, length, width + states), BF16),
        in_specs=[
            SMEM,
            pl.BlockSpec((1, length, heads), lambda r: (r, 0, 0)),
            pl.BlockSpec((1, length, width), lambda r: (r, 0, 0)),
            pl.BlockSpec((1, length, states), lambda r: (r, 0, 0)),
        ],
        out_specs=pl.BlockSpec((1, length, width + states), lambda r: (r, 0, 0)),
        name="carry_cotangent",
    )(resp_length, log_decay, out_cotangent, state_out)


def distance_to(rank, owner, devices):
    gap = rank - owner
    return jnp.where(gap < 0, gap + devices, gap)


def mamba_kernel(
    devices,
    rank_ref,
    resp_prefix,
    resp_length,
    skip_gain,
    inputs,
    pack0,
    pack1,
    pack2,
    pack3,
    conv_weight,
    write,
    read,
    log_decay,
    cotangent,
    g_inputs,
    g_tail,
    g_conv,
    g_read,
    padded,
    shifted,
    tail_rows,
    inner,
):
    resp = pl.program_id(0)
    length = inputs.shape[1]
    width = inputs.shape[2]
    taps = conv_weight.shape[0]
    rank = rank_ref[0]
    live_to = resp_length[resp]
    gap = distance_to(rank, resp_prefix[2 * rank + resp], devices)
    for step, packed in enumerate((pack0, pack1, pack2, pack3)):

        @pl.when(gap == step)
        def _(packed=packed):
            for half in range(2):
                tail_rows[half] = packed[half, length : length + 16, :].astype(F32)

    for part in range(4):
        padded[0:8, part * 512 : part * 512 + 512] = tail_rows[part // 2, 8 * (part % 2) : 8 * (part % 2) + 8, :]
    padded[8 : 8 + length, :] = inputs[0].astype(F32)
    decay_sum = running_sum(log_decay[0])
    decay_rows = jnp.concatenate(
        [decay_sum, jnp.zeros((length, 128 - decay_sum.shape[1]), F32)], axis=1
    ).T
    s_index = lax.broadcasted_iota(jnp.int32, (length, length), 0)
    t_index = lax.broadcasted_iota(jnp.int32, (length, length), 1)
    causal = s_index <= t_index
    mixing = nt(write[0], read[0])
    live = lax.broadcasted_iota(jnp.int32, (length, 2 * HEAD_DIM), 0) < live_to
    first = lax.broadcasted_iota(jnp.int32, (length, 2 * HEAD_DIM), 1) < HEAD_DIM
    inner[...] = jnp.zeros_like(inner)
    for pair in range(width // (2 * HEAD_DIM)):
        lo = pair * 2 * HEAD_DIM
        lanes = slice(lo, lo + 2 * HEAD_DIM)
        weight = [conv_weight[k : k + 1, lanes] for k in range(taps)]
        mixed = weight[0] * padded[5 : 5 + length, lanes]
        for k in range(1, taps):
            mixed = mixed + weight[k] * padded[5 + k : 5 + k + length, lanes]
        gate = jax.nn.sigmoid(mixed)
        activated = (mixed * gate).astype(BF16)
        d_out = jnp.where(live, cotangent[0, :, lanes].astype(F32), 0.0)
        both = jnp.concatenate(
            [jnp.where(first, d_out, 0.0).astype(BF16), jnp.where(first, 0.0, d_out).astype(BF16)], axis=0
        )
        d_weights = nt(activated, both)
        decays = []
        for head in (2 * pair, 2 * pair + 1):
            lag = decay_rows[head : head + 1, :] - decay_sum[:, head : head + 1]
            decays.append(jnp.exp(jnp.where(causal, lag, NEG_FILL)))
        weights = jnp.concatenate([(d * mixing).astype(BF16) for d in decays], axis=1)
        inner[...] += decays[0] * d_weights[:, :length] + decays[1] * d_weights[:, length:]
        gain = jnp.where(first[0:1], skip_gain[2 * pair], skip_gain[2 * pair + 1])
        d_act = nn(weights, both) + gain * d_out
        d_mixed = d_act * (gate * (1.0 + mixed * (1.0 - gate)))
        shifted[0:8, lanes] = jnp.zeros((8, 2 * HEAD_DIM), F32)
        shifted[8 : 8 + length, lanes] = d_mixed
        shifted[8 + length : 16 + length, lanes] = jnp.zeros((8, 2 * HEAD_DIM), F32)
        total = weight[0] * shifted[11 : 11 + length, lanes]
        early = weight[0] * shifted[8:16, lanes]
        for k in range(1, taps):
            total = total + weight[k] * shifted[11 - k : 11 - k + length, lanes]
            early = early + weight[k] * shifted[8 - k : 16 - k, lanes]
        g_inputs[0, :, lanes] = total.astype(BF16)
        g_tail[0, lo // 512, :, lo % 512 : lo % 512 + 2 * HEAD_DIM] = early
        rows = [
            jnp.sum(d_mixed * padded[5 + k : 5 + k + length, lanes], axis=0, keepdims=True) for k in range(taps)
        ]
        rows = jnp.concatenate(rows, axis=0)

        @pl.when(resp == 0)
        def _(rows=rows, lanes=lanes):
            g_conv[:, lanes] = rows

        @pl.when(resp > 0)
        def _(rows=rows, lanes=lanes):
            g_conv[:, lanes] += rows

    g_read[0] = tn(inner[...].astype(BF16), write[0])


def mamba(rank, resp_prefix, resp_length, skip_gain, inputs, packs, conv_weight, write, read, log_decay, cotangent, devices):
    count, length, width = inputs.shape
    heads = log_decay.shape[2]
    states = read.shape[2]
    taps = conv_weight.shape[0]
    whole = pl.BlockSpec(packs[0].shape, lambda r: (0, 0, 0))
    return pl.pallas_call(
        functools.partial(mamba_kernel, devices),
        grid=(count,),
        out_shape=[
            jax.ShapeDtypeStruct((count, length, width), BF16),
            jax.ShapeDtypeStruct((count, 4, 8, 512), F32),
            jax.ShapeDtypeStruct((taps, width), F32),
            jax.ShapeDtypeStruct((count, length, states), F32),
        ],
        in_specs=[
            SMEM,
            SMEM,
            SMEM,
            SMEM,
            pl.BlockSpec((1, length, width), lambda r: (r, 0, 0)),
            whole,
            whole,
            whole,
            whole,
            pl.BlockSpec((taps, width), lambda r: (0, 0)),
            pl.BlockSpec((1, length, states), lambda r: (r, 0, 0)),
            pl.BlockSpec((1, length, states), lambda r: (r, 0, 0)),
            pl.BlockSpec((1, length, heads), lambda r: (r, 0, 0)),
            pl.BlockSpec((1, length, width), lambda r: (r, 0, 0)),
        ],
        out_specs=[
            pl.BlockSpec((1, length, width), lambda r: (r, 0, 0)),
            pl.BlockSpec((1, 4, 8, 512), lambda r: (r, 0, 0, 0)),
            pl.BlockSpec((taps, width), lambda r: (0, 0)),
            pl.BlockSpec((1, length, states), lambda r: (r, 0, 0)),
        ],
        scratch_shapes=[
            pltpu.VMEM((length + 8, width), F32),
            pltpu.VMEM((length + 16, width), F32),
            pltpu.VMEM((2, 16, 512), F32),
            pltpu.VMEM((length, length), F32),
        ],
        compiler_params=pltpu.CompilerParams(vmem_limit_bytes=32 * 2**20),
        cost_estimate=pl.CostEstimate(flops=2 * 10**9, bytes_accessed=8 * 2**20, transcendentals=10**6),
        name="mamba_grads",
    )(rank, resp_prefix, resp_length, skip_gain, inputs, *packs, conv_weight, write, read, log_decay, cotangent)


def attention_kernel(
    devices,
    rank_ref,
    resp_prefix,
    resp_length,
    prefix_length,
    queries,
    cotangent,
    own_keys,
    own_values,
    pack0,
    pack1,
    pack2,
    pack3,
    g_tail,
    g_queries,
    back0,
    back1,
    back2,
    back3,
    keys,
    values,
    kept,
):
    resp = pl.program_id(1)
    length = queries.shape[1]
    rows = keys.shape[0] - length
    rank = rank_ref[0]
    prefix = resp_prefix[2 * rank + resp]
    pref_len = prefix_length[prefix]
    live_to = resp_length[resp]
    scale = 1.0 / math.sqrt(ATT_DIM)
    gap = distance_to(rank, prefix, devices)
    for step, packed in enumerate((pack0, pack1, pack2, pack3)):

        @pl.when(gap == step)
        def _(packed=packed):
            keys[0:rows, :] = packed[0, 0:rows, :]
            values[0:rows, :] = packed[1, 0:rows, :]

    keys[rows : rows + length, :] = own_keys[0]
    values[rows : rows + length, :] = own_values[0]
    j_index = lax.broadcasted_iota(jnp.int32, (rows + length, 2 * length), 0)
    t_index = lax.broadcasted_iota(jnp.int32, (rows + length, 2 * length), 1)
    t_index = jnp.where(t_index >= length, t_index - length, t_index)
    bound = jnp.where(j_index < rows, pref_len, t_index + rows + 1)
    bias = jnp.where(j_index < bound, 0.0, NEG_FILL)
    live = lax.broadcasted_iota(jnp.int32, (length, ATT_DIM), 0) < live_to
    all_keys = keys[...]
    all_values = values[...]
    g_keys = jnp.zeros((rows, ATT_DIM), F32)
    g_values = jnp.zeros((rows, ATT_DIM), F32)
    for duo in range(REPEAT // 2):
        spans = [slice((2 * duo + i) * ATT_DIM, (2 * duo + i + 1) * ATT_DIM) for i in range(2)]
        query = jnp.concatenate([queries[0, :, span] for span in spans], axis=0)
        d_out = jnp.concatenate(
            [jnp.where(live, cotangent[0, :, span].astype(F32), 0.0).astype(BF16) for span in spans], axis=0
        )
        scores = nt(all_keys, query) * scale + bias
        top = jnp.max(scores, axis=0, keepdims=True)
        raised = jnp.exp(scores - top)
        probs = raised * (1.0 / jnp.sum(raised, axis=0, keepdims=True))
        probs_low = probs.astype(BF16)
        d_probs = nt(all_values, d_out)
        delta = jnp.sum(probs_low.astype(F32) * d_probs, axis=0, keepdims=True)
        d_scores = (probs * ((d_probs - delta) * scale)).astype(BF16)
        g_query = tn(d_scores, all_keys)
        for i, span in enumerate(spans):
            g_queries[0, :, span] = g_query[i * length : (i + 1) * length].astype(BF16)
        g_keys = g_keys + nn(d_scores[0:rows], query)
        g_values = g_values + nn(probs_low[0:rows], d_out)

    @pl.when(resp == 0)
    def _():
        kept[0] = g_keys
        kept[1] = g_values

    @pl.when(resp == 1)
    def _():
        before = distance_to(rank, resp_prefix[2 * rank], devices)
        for step, back in enumerate((back0, back1, back2, back3)):
            one = jnp.where(before == step, 1.0, 0.0)
            two = jnp.where(gap == step, 1.0, 0.0)
            back[0, 0:rows, :] = (kept[0] * one + g_keys * two).astype(back.dtype)
            back[1, 0:rows, :] = (kept[1] * one + g_values * two).astype(back.dtype)
            for half in range(2):
                upper = g_tail[0, 2 * half] * one + g_tail[1, 2 * half] * two
                lower = g_tail[0, 2 * half + 1] * one + g_tail[1, 2 * half + 1] * two
                back[half, rows : rows + 16, :] = jnp.concatenate([upper, lower], axis=0).astype(back.dtype)


def attention(rank, resp_prefix, resp_length, prefix_length, queries, cotangent, own_keys, own_values, packs, g_tail, devices):
    count, length, width = queries.shape
    rows = packs[0].shape[1] - 16
    group = REPEAT * ATT_DIM
    packed = pl.BlockSpec((2, rows + 16, ATT_DIM), lambda h, r: (0, 0, h))
    back = (2, rows + 16, KV_HEADS * ATT_DIM)
    return pl.pallas_call(
        functools.partial(attention_kernel, devices),
        grid=(KV_HEADS, count),
        out_shape=[
            jax.ShapeDtypeStruct((count, length, width), BF16),
            jax.ShapeDtypeStruct(back, F32),
            jax.ShapeDtypeStruct(back, BF16),
            jax.ShapeDtypeStruct(back, BF16),
            jax.ShapeDtypeStruct(back, BF16),
        ],
        in_specs=[
            SMEM,
            SMEM,
            SMEM,
            SMEM,
            pl.BlockSpec((1, length, group), lambda h, r: (r, 0, h)),
            pl.BlockSpec((1, length, group), lambda h, r: (r, 0, h)),
            pl.BlockSpec((1, length, ATT_DIM), lambda h, r: (r, 0, h)),
            pl.BlockSpec((1, length, ATT_DIM), lambda h, r: (r, 0, h)),
            packed,
            packed,
            packed,
            packed,
            pl.BlockSpec((count, 4, 8, ATT_DIM), lambda h, r: (0, 0, 0, h)),
        ],
        out_specs=[
            pl.BlockSpec((1, length, group), lambda h, r: (r, 0, h)),
            packed,
            packed,
            packed,
            packed,
        ],
        scratch_shapes=[
            pltpu.VMEM((rows + length, ATT_DIM), BF16),
            pltpu.VMEM((rows + length, ATT_DIM), BF16),
            pltpu.VMEM((2, rows, ATT_DIM), F32),
        ],
        compiler_params=pltpu.CompilerParams(vmem_limit_bytes=32 * 2**20),
        cost_estimate=pl.CostEstimate(flops=4 * 10**9, bytes_accessed=8 * 2**20, transcendentals=2 * 10**6),
        name="attention_grads",
    )(rank, resp_prefix, resp_length, prefix_length, queries, cotangent, own_keys, own_values, *packs, g_tail)


def owner_kernel(devices, rank_ref, resp_prefix, state, car0, car1, car2, car3, g_state, dr0, dr1, dr2, dr3, total):
    rank = rank_ref[0]
    width = state.shape[0]
    chunk = 512
    total[...] = jnp.zeros_like(total)
    for step, (carried, d_read) in enumerate(zip((car0, car1, car2, car3), (dr0, dr1, dr2, dr3))):
        sender = rank + step
        sender = jnp.where(sender >= devices, sender - devices, sender)
        for resp in range(2):
            mine = resp_prefix[2 * sender + resp] == rank

            @pl.when(mine)
            def _(carried=carried, d_read=d_read, resp=resp):
                read = carried[resp, :, width:]
                acc = None
                for at in range(0, width, chunk):
                    piece = carried[resp, :, at : at + chunk]
                    term = nn(piece, state[at : at + chunk, :])
                    acc = term if acc is None else acc + term
                    total[at : at + chunk, :] += tn(piece, read)
                d_read[resp] = acc.astype(d_read.dtype)

            @pl.when(jnp.logical_not(mine))
            def _(d_read=d_read, resp=resp):
                d_read[resp] = jnp.zeros(d_read.shape[1:], d_read.dtype)

    g_state[...] = total[...].astype(BF16)


def owner(rank, resp_prefix, state, carried, devices):
    width, states = state.shape
    count, length = carried[0].shape[:2]
    return pl.pallas_call(
        functools.partial(owner_kernel, devices),
        out_shape=[jax.ShapeDtypeStruct((width, states), BF16), jax.ShapeDtypeStruct((count, length, states), F32)]
        + [jax.ShapeDtypeStruct((count, length, states), BF16)] * 3,
        in_specs=[SMEM, SMEM] + [VMEM] * 5,
        out_specs=[VMEM] * 5,
        scratch_shapes=[pltpu.VMEM((width, states), F32)],
        compiler_params=pltpu.CompilerParams(vmem_limit_bytes=32 * 2**20),
        cost_estimate=pl.CostEstimate(flops=2 * 10**9, bytes_accessed=8 * 2**20, transcendentals=0),
        name="owner_state",
    )(rank, resp_prefix, state, *carried)


def sum_kernel(back0, back1, back2, back3, g_keys, g_values, g_tail):
    rows = g_keys.shape[1]
    for half, out in enumerate((g_keys, g_values)):
        total = back0[half]
        for back in (back1, back2, back3):
            total = total + back[half].astype(F32)
        out[0] = total[0:rows]
        for part in range(2):
            lo = half * 1024 + part * 512
            g_tail[0, :, lo : lo + 512] = total[rows + 8 * part : rows + 8 * part + 3]


def sum_back(backs, tail_shape):
    rows = backs[0].shape[1] - 16
    width = backs[0].shape[2]
    return pl.pallas_call(
        sum_kernel,
        out_shape=[
            jax.ShapeDtypeStruct((1, rows, width), F32),
            jax.ShapeDtypeStruct((1, rows, width), F32),
            jax.ShapeDtypeStruct(tail_shape, F32),
        ],
        in_specs=[VMEM] * 4,
        out_specs=[VMEM] * 3,
        name="sum_prefix",
    )(*backs)


def all_sum(value):
    length = lax.axis_size("dp")
    if length & (length - 1):
        return lax.psum(value, "dp")
    by = 1
    while by < length:
        value = value + lax.ppermute(value, "dp", [(i, i ^ by) for i in range(length)])
        by *= 2
    return value


def on_device(
    token_inputs,
    state_in,
    state_out,
    log_decay,
    skip_gain,
    conv_weight,
    out_cotangent,
    queries,
    own_keys,
    own_values,
    attn_cotangent,
    resp_length,
    resp_prefix,
    prefix_state,
    prefix_tail,
    prefix_keys,
    prefix_values,
    prefix_length,
):
    devices = lax.axis_size("dp")
    rank = lax.axis_index("dp").astype(jnp.int32).reshape(1)
    count, length, _ = token_inputs.shape
    states = state_out.shape[3]
    write = state_in.reshape(count, length, states)
    read = state_out.reshape(count, length, states)
    state = prefix_state.reshape(-1, states)

    packed = pack(prefix_keys, prefix_values, prefix_tail)
    packs = [packed] + [shift(packed, by) for by in range(1, SPAN)]
    carried = carry(resp_length, log_decay, out_cotangent, read)
    carries = [carried] + [shift(carried, -by) for by in range(1, SPAN)]
    g_inputs, g_tail, g_conv, g_read = mamba(
        rank, resp_prefix, resp_length, skip_gain, token_inputs, packs, conv_weight, write, read, log_decay, out_cotangent, devices
    )
    g_queries, *backs = attention(
        rank, resp_prefix, resp_length, prefix_length, queries, attn_cotangent, own_keys, own_values, packs, g_tail, devices
    )
    backs = [backs[0]] + [shift(backs[by], -by) for by in range(1, SPAN)]
    g_state, *reads = owner(rank, resp_prefix, state, carries, devices)
    for by in range(SPAN):
        g_read = g_read + (reads[by] if by == 0 else shift(reads[by], by).astype(F32))
    g_prefix_keys, g_prefix_values, g_prefix_tail = sum_back(backs, prefix_tail.shape)
    token_total = count * length * devices
    grad_conv = all_sum(g_conv) * (1.0 / math.sqrt(token_total))
    return (
        g_inputs,
        g_read.astype(BF16).reshape(state_out.shape),
        g_queries,
        g_state.reshape(prefix_state.shape),
        g_prefix_tail,
        g_prefix_keys,
        g_prefix_values,
        grad_conv,
    )


def solution(mesh):
    split = ("groups", "dp")
    placed = (
        P(split, None, None),
        P(split, None, None, None),
        P(split, None, None, None),
        P(split, None, None),
        P(),
        P(),
        P(split, None, None),
        P(split, None, None),
        P(split, None, None),
        P(split, None, None),
        P(split, None, None),
        P(split),
        P("groups"),
        P(split, None, None, None),
        P(split, None, None),
        P(split, None, None),
        P(split, None, None),
        P("groups"),
    )
    return jax.shard_map(
        on_device,
        mesh=mesh,
        in_specs=placed,
        out_specs=(
            P(split, None, None),
            P(split, None, None, None),
            P(split, None, None),
            P(split, None, None, None),
            P(split, None, None),
            P(split, None, None),
            P(split, None, None),
            P("groups", None),
        ),
        check_vma=False,
    )
```

```python
import functools
import math

import jax
import jax.numpy as jnp
from jax import lax
from jax.experimental import pallas as pl
from jax.experimental.pallas import tpu as pltpu
from jax.sharding import PartitionSpec as P

ATT_HEADS = 32
KV_HEADS = 4
ATT_DIM = 128
HEADS = 32
HEAD_DIM = 64
SPAN = 4
REPEAT = ATT_HEADS // KV_HEADS
NEG_FILL = -1e30
F32 = jnp.float32
BF16 = jnp.bfloat16

SMEM = pl.BlockSpec(memory_space=pltpu.SMEM)
VMEM = pl.BlockSpec(memory_space=pltpu.VMEM)


def shift(value, by):
    length = lax.axis_size("dp")
    return lax.ppermute(value, "dp", [(i, (i + by) % length) for i in range(length)])


def nt(a, b):
    return lax.dot_general(a, b, (((1,), (1,)), ((), ())), preferred_element_type=F32)


def tn(a, b):
    return lax.dot_general(a, b, (((0,), (0,)), ((), ())), preferred_element_type=F32)


def nn(a, b):
    return lax.dot_general(a, b, (((1,), (0,)), ((), ())), preferred_element_type=F32)


def pack_kernel(keys, values, out):
    out[0] = keys[0]
    out[1] = values[0]


def pack(prefix_keys, prefix_values):
    return pl.pallas_call(
        pack_kernel,
        out_shape=jax.ShapeDtypeStruct((2,) + prefix_keys.shape[1:], BF16),
        in_specs=[VMEM] * 2,
        out_specs=VMEM,
        name="pack_prefix",
    )(prefix_keys, prefix_values)


def running_sum(log_decay):
    heads, length = log_decay.shape
    row = lax.broadcasted_iota(jnp.int32, (length, length), 0)
    col = lax.broadcasted_iota(jnp.int32, (length, length), 1)
    upper = (row <= col).astype(F32)
    rows = lax.dot_general(
        log_decay,
        upper,
        (((1,), (0,)), ((), ())),
        precision=lax.Precision.HIGHEST,
        preferred_element_type=F32,
    )
    return jnp.concatenate([rows, jnp.zeros((128 - heads, length), F32)], axis=0).T, rows


def carry_kernel(resp_length, log_decay, cotangent, read, out):
    length = cotangent.shape[1]
    width = cotangent.shape[2]
    live_to = resp_length[pl.program_id(0)]
    raised = jnp.exp(running_sum(log_decay[0])[0])
    live = lax.broadcasted_iota(jnp.int32, (length, 2 * HEAD_DIM), 0) < live_to
    first = lax.broadcasted_iota(jnp.int32, (length, 2 * HEAD_DIM), 1) < HEAD_DIM
    for pair in range(width // (2 * HEAD_DIM)):
        lanes = slice(pair * 2 * HEAD_DIM, (pair + 1) * 2 * HEAD_DIM)
        factor = jnp.where(first, raised[:, 2 * pair : 2 * pair + 1], raised[:, 2 * pair + 1 : 2 * pair + 2])
        factor = jnp.where(live, factor, 0.0)
        out[0, :, lanes] = (factor * cotangent[0, :, lanes].astype(F32)).astype(BF16)
    out[0, :, width:] = read[0]


def carry(resp_length, log_decay, out_cotangent, state_out):
    count, length, width = out_cotangent.shape
    heads = log_decay.shape[1]
    states = state_out.shape[2]
    return pl.pallas_call(
        carry_kernel,
        grid=(count,),
        out_shape=jax.ShapeDtypeStruct((count, length, width + states), BF16),
        in_specs=[
            SMEM,
            pl.BlockSpec((1, heads, length), lambda r: (r, 0, 0)),
            pl.BlockSpec((1, length, width), lambda r: (r, 0, 0)),
            pl.BlockSpec((1, length, states), lambda r: (r, 0, 0)),
        ],
        out_specs=pl.BlockSpec((1, length, width + states), lambda r: (r, 0, 0)),
        name="carry_cotangent",
    )(resp_length, log_decay, out_cotangent, state_out)


def relayed(rank):
    even = rank % 2 == 0
    return 0, 2, jnp.where(even, 1, 3), jnp.where(even, 3, 1)


def gather(value, sign):
    length = lax.axis_size("dp")
    two = shift(value, 2 * sign)
    if sign > 0:
        pairs = [(i, (i + (3 if i % 2 else 1)) % length) for i in range(length)]
    else:
        pairs = [(i, (i - (1 if i % 2 else 3)) % length) for i in range(length)]
    last = lax.ppermute(value, "dp", pairs)
    return [value, two, lax.ppermute(two, "dp", [(i, i ^ 1) for i in range(length)]), last]


def distance_to(rank, owner, devices):
    gap = rank - owner
    return jnp.where(gap < 0, gap + devices, gap)


def mamba_kernel(
    devices,
    rank_ref,
    resp_prefix,
    resp_length,
    skip_gain,
    inputs,
    tail0,
    tail1,
    tail2,
    tail3,
    conv_weight,
    write,
    read,
    log_decay,
    cotangent,
    g_inputs,
    g_tail,
    g_conv,
    g_read,
    padded,
    shifted,
    inner,
):
    resp = pl.program_id(0)
    length = inputs.shape[1]
    width = inputs.shape[2]
    taps = conv_weight.shape[0]
    rank = rank_ref[0]
    live_to = resp_length[resp]
    gap = distance_to(rank, resp_prefix[2 * rank + resp], devices)
    for step, tail in enumerate((tail0, tail1, tail2, tail3)):

        @pl.when(gap == step)
        def _(tail=tail):
            padded[5:8, :] = tail[0].astype(F32)

    padded[8 : 8 + length, :] = inputs[0].astype(F32)
    decay_sum, decay_rows = running_sum(log_decay[0])
    s_index = lax.broadcasted_iota(jnp.int32, (length, length), 0)
    t_index = lax.broadcasted_iota(jnp.int32, (length, length), 1)
    causal = s_index <= t_index
    mixing = nt(write[0], read[0])
    live = lax.broadcasted_iota(jnp.int32, (length, 2 * HEAD_DIM), 0) < live_to
    first = lax.broadcasted_iota(jnp.int32, (length, 2 * HEAD_DIM), 1) < HEAD_DIM
    inner[...] = jnp.zeros_like(inner)
    for pair in range(width // (2 * HEAD_DIM)):
        lo = pair * 2 * HEAD_DIM
        lanes = slice(lo, lo + 2 * HEAD_DIM)
        weight = [conv_weight[k : k + 1, lanes] for k in range(taps)]
        mixed = weight[0] * padded[5 : 5 + length, lanes]
        for k in range(1, taps):
            mixed = mixed + weight[k] * padded[5 + k : 5 + k + length, lanes]
        gate = jax.nn.sigmoid(mixed)
        activated = (mixed * gate).astype(BF16)
        d_out = jnp.where(live, cotangent[0, :, lanes].astype(F32), 0.0)
        both = jnp.concatenate(
            [jnp.where(first, d_out, 0.0).astype(BF16), jnp.where(first, 0.0, d_out).astype(BF16)], axis=0
        )
        d_weights = nt(activated, both)
        decays = []
        for head in (2 * pair, 2 * pair + 1):
            lag = decay_rows[head : head + 1, :] - decay_sum[:, head : head + 1]
            decays.append(jnp.exp(jnp.where(causal, lag, NEG_FILL)))
        weights = jnp.concatenate([(d * mixing).astype(BF16) for d in decays], axis=1)
        inner[...] += decays[0] * d_weights[:, :length] + decays[1] * d_weights[:, length:]
        gain = jnp.where(first[0:1], skip_gain[2 * pair], skip_gain[2 * pair + 1])
        d_act = nn(weights, both) + gain * d_out
        d_mixed = d_act * (gate * (1.0 + mixed * (1.0 - gate)))
        shifted[0:8, lanes] = jnp.zeros((8, 2 * HEAD_DIM), F32)
        shifted[8 : 8 + length, lanes] = d_mixed
        shifted[8 + length : 16 + length, lanes] = jnp.zeros((8, 2 * HEAD_DIM), F32)
        total = weight[0] * shifted[11 : 11 + length, lanes]
        early = weight[0] * shifted[8:16, lanes]
        for k in range(1, taps):
            total = total + weight[k] * shifted[11 - k : 11 - k + length, lanes]
            early = early + weight[k] * shifted[8 - k : 16 - k, lanes]
        g_inputs[0, :, lanes] = total.astype(BF16)
        g_tail[0, lo // 512, :, lo % 512 : lo % 512 + 2 * HEAD_DIM] = early
        rows = [
            jnp.sum(d_mixed * padded[5 + k : 5 + k + length, lanes], axis=0, keepdims=True) for k in range(taps)
        ]
        rows = jnp.concatenate(rows, axis=0)

        @pl.when(resp == 0)
        def _(rows=rows, lanes=lanes):
            g_conv[:, lanes] = rows

        @pl.when(resp > 0)
        def _(rows=rows, lanes=lanes):
            g_conv[:, lanes] += rows

    g_read[0] = tn(inner[...].astype(BF16), write[0])


def mamba(rank, resp_prefix, resp_length, skip_gain, inputs, tails, conv_weight, write, read, log_decay, cotangent, devices):
    count, length, width = inputs.shape
    heads = log_decay.shape[1]
    states = read.shape[2]
    taps = conv_weight.shape[0]
    whole = pl.BlockSpec(tails[0].shape, lambda r: (0, 0, 0))
    return pl.pallas_call(
        functools.partial(mamba_kernel, devices),
        grid=(count,),
        out_shape=[
            jax.ShapeDtypeStruct((count, length, width), BF16),
            jax.ShapeDtypeStruct((count, 4, 8, 512), F32),
            jax.ShapeDtypeStruct((taps, width), F32),
            jax.ShapeDtypeStruct((count, length, states), F32),
        ],
        in_specs=[
            SMEM,
            SMEM,
            SMEM,
            SMEM,
            pl.BlockSpec((1, length, width), lambda r: (r, 0, 0)),
            whole,
            whole,
            whole,
            whole,
            pl.BlockSpec((taps, width), lambda r: (0, 0)),
            pl.BlockSpec((1, length, states), lambda r: (r, 0, 0)),
            pl.BlockSpec((1, length, states), lambda r: (r, 0, 0)),
            pl.BlockSpec((1, heads, length), lambda r: (r, 0, 0)),
            pl.BlockSpec((1, length, width), lambda r: (r, 0, 0)),
        ],
        out_specs=[
            pl.BlockSpec((1, length, width), lambda r: (r, 0, 0)),
            pl.BlockSpec((1, 4, 8, 512), lambda r: (r, 0, 0, 0)),
            pl.BlockSpec((taps, width), lambda r: (0, 0)),
            pl.BlockSpec((1, length, states), lambda r: (r, 0, 0)),
        ],
        scratch_shapes=[
            pltpu.VMEM((length + 8, width), F32),
            pltpu.VMEM((length + 16, width), F32),
            pltpu.VMEM((length, length), F32),
        ],
        compiler_params=pltpu.CompilerParams(vmem_limit_bytes=32 * 2**20),
        cost_estimate=pl.CostEstimate(flops=2 * 10**9, bytes_accessed=8 * 2**20, transcendentals=10**6),
        name="mamba_grads",
    )(rank, resp_prefix, resp_length, skip_gain, inputs, *tails, conv_weight, write, read, log_decay, cotangent)


def attention_kernel(
    devices,
    rank_ref,
    resp_prefix,
    resp_length,
    prefix_length,
    queries,
    cotangent,
    own_keys,
    own_values,
    pack0,
    pack1,
    pack2,
    pack3,
    g_tail,
    g_queries,
    back0,
    back1,
    back2,
    back3,
    keys,
    values,
    kept,
):
    resp = pl.program_id(1)
    length = queries.shape[1]
    rows = keys.shape[0] - length
    rank = rank_ref[0]
    prefix = resp_prefix[2 * rank + resp]
    pref_len = prefix_length[prefix]
    live_to = resp_length[resp]
    scale = 1.0 / math.sqrt(ATT_DIM)
    gap = distance_to(rank, prefix, devices)
    for step, packed in zip(relayed(rank), (pack0, pack1, pack2, pack3)):

        @pl.when(gap == step)
        def _(packed=packed):
            keys[0:rows, :] = packed[0, 0:rows, :]
            values[0:rows, :] = packed[1, 0:rows, :]

    keys[rows : rows + length, :] = own_keys[0]
    values[rows : rows + length, :] = own_values[0]
    j_index = lax.broadcasted_iota(jnp.int32, (rows + length, 2 * length), 0)
    t_index = lax.broadcasted_iota(jnp.int32, (rows + length, 2 * length), 1)
    t_index = jnp.where(t_index >= length, t_index - length, t_index)
    bound = jnp.where(j_index < rows, pref_len, t_index + rows + 1)
    bias = jnp.where(j_index < bound, 0.0, NEG_FILL)
    live = lax.broadcasted_iota(jnp.int32, (length, ATT_DIM), 0) < live_to
    all_keys = keys[...]
    all_values = values[...]
    g_keys = jnp.zeros((rows, ATT_DIM), F32)
    g_values = jnp.zeros((rows, ATT_DIM), F32)
    for duo in range(REPEAT // 2):
        spans = [slice((2 * duo + i) * ATT_DIM, (2 * duo + i + 1) * ATT_DIM) for i in range(2)]
        query = jnp.concatenate([queries[0, :, span] for span in spans], axis=0)
        d_out = jnp.concatenate(
            [jnp.where(live, cotangent[0, :, span].astype(F32), 0.0).astype(BF16) for span in spans], axis=0
        )
        scores = nt(all_keys, query) * scale + bias
        top = jnp.max(scores, axis=0, keepdims=True)
        raised = jnp.exp(scores - top)
        probs = raised * (1.0 / jnp.sum(raised, axis=0, keepdims=True))
        probs_low = probs.astype(BF16)
        d_probs = nt(all_values, d_out)
        delta = jnp.sum(probs_low.astype(F32) * d_probs, axis=0, keepdims=True)
        d_scores = (probs * ((d_probs - delta) * scale)).astype(BF16)
        g_query = tn(d_scores, all_keys)
        for i, span in enumerate(spans):
            g_queries[0, :, span] = g_query[i * length : (i + 1) * length].astype(BF16)
        g_keys = g_keys + nn(d_scores[0:rows], query)
        g_values = g_values + nn(probs_low[0:rows], d_out)

    @pl.when(resp == 0)
    def _():
        kept[0] = g_keys
        kept[1] = g_values

    @pl.when(resp == 1)
    def _():
        before = distance_to(rank, resp_prefix[2 * rank], devices)
        for step, back in enumerate((back0, back1, back2, back3)):
            one = jnp.where(before == step, 1.0, 0.0)
            two = jnp.where(gap == step, 1.0, 0.0)
            back[0, 0:rows, :] = (kept[0] * one + g_keys * two).astype(back.dtype)
            back[1, 0:rows, :] = (kept[1] * one + g_values * two).astype(back.dtype)
            for half in range(2):
                upper = g_tail[0, 2 * half] * one + g_tail[1, 2 * half] * two
                lower = g_tail[0, 2 * half + 1] * one + g_tail[1, 2 * half + 1] * two
                back[half, rows : rows + 16, :] = jnp.concatenate([upper, lower], axis=0).astype(back.dtype)


def attention(rank, resp_prefix, resp_length, prefix_length, queries, cotangent, own_keys, own_values, packs, g_tail, devices):
    count, length, width = queries.shape
    rows = packs[0].shape[1]
    group = REPEAT * ATT_DIM
    packed = pl.BlockSpec((2, rows, ATT_DIM), lambda h, r: (0, 0, h))
    back_block = pl.BlockSpec((2, rows + 16, ATT_DIM), lambda h, r: (0, 0, h))
    back = (2, rows + 16, KV_HEADS * ATT_DIM)
    return pl.pallas_call(
        functools.partial(attention_kernel, devices),
        grid=(KV_HEADS, count),
        out_shape=[
            jax.ShapeDtypeStruct((count, length, width), BF16),
            jax.ShapeDtypeStruct(back, F32),
            jax.ShapeDtypeStruct(back, BF16),
            jax.ShapeDtypeStruct(back, BF16),
            jax.ShapeDtypeStruct(back, BF16),
        ],
        in_specs=[
            SMEM,
            SMEM,
            SMEM,
            SMEM,
            pl.BlockSpec((1, length, group), lambda h, r: (r, 0, h)),
            pl.BlockSpec((1, length, group), lambda h, r: (r, 0, h)),
            pl.BlockSpec((1, length, ATT_DIM), lambda h, r: (r, 0, h)),
            pl.BlockSpec((1, length, ATT_DIM), lambda h, r: (r, 0, h)),
            packed,
            packed,
            packed,
            packed,
            pl.BlockSpec((count, 4, 8, ATT_DIM), lambda h, r: (0, 0, 0, h)),
        ],
        out_specs=[
            pl.BlockSpec((1, length, group), lambda h, r: (r, 0, h)),
            back_block,
            back_block,
            back_block,
            back_block,
        ],
        scratch_shapes=[
            pltpu.VMEM((rows + length, ATT_DIM), BF16),
            pltpu.VMEM((rows + length, ATT_DIM), BF16),
            pltpu.VMEM((2, rows, ATT_DIM), F32),
        ],
        compiler_params=pltpu.CompilerParams(vmem_limit_bytes=32 * 2**20),
        cost_estimate=pl.CostEstimate(flops=4 * 10**9, bytes_accessed=8 * 2**20, transcendentals=2 * 10**6),
        name="attention_grads",
    )(rank, resp_prefix, resp_length, prefix_length, queries, cotangent, own_keys, own_values, *packs, g_tail)


def owner_kernel(devices, rank_ref, resp_prefix, state, car0, car1, car2, car3, g_state, dr0, dr1, dr2, dr3, total, parts):
    rank = rank_ref[0]
    even = rank % 2 == 0
    width = state.shape[0]
    chunk = 512
    total[...] = jnp.zeros_like(total)
    for slot, (step, carried) in enumerate(
        zip((0, 2, jnp.where(even, 3, 1), jnp.where(even, 1, 3)), (car0, car1, car2, car3))
    ):
        sender = rank + step
        sender = jnp.where(sender >= devices, sender - devices, sender)
        for resp in range(2):
            mine = resp_prefix[2 * sender + resp] == rank

            @pl.when(mine)
            def _(carried=carried, slot=slot, resp=resp):
                read = carried[resp, :, width:]
                acc = None
                for at in range(0, width, chunk):
                    piece = carried[resp, :, at : at + chunk]
                    term = nn(piece, state[at : at + chunk, :])
                    acc = term if acc is None else acc + term
                    total[at : at + chunk, :] += tn(piece, read)
                parts[slot, resp] = acc

            @pl.when(jnp.logical_not(mine))
            def _(slot=slot, resp=resp):
                parts[slot, resp] = jnp.zeros(parts.shape[2:], F32)

    g_state[...] = total[...].astype(BF16)
    dr0[...] = parts[0]
    dr2[...] = parts[1].astype(BF16)

    @pl.when(even)
    def _():
        dr3[...] = parts[2].astype(BF16)
        dr1[...] = parts[3].astype(BF16)

    @pl.when(jnp.logical_not(even))
    def _():
        dr1[...] = parts[2].astype(BF16)
        dr3[...] = parts[3].astype(BF16)


def owner(rank, resp_prefix, state, carried, devices):
    width, states = state.shape
    count, length = carried[0].shape[:2]
    return pl.pallas_call(
        functools.partial(owner_kernel, devices),
        out_shape=[jax.ShapeDtypeStruct((width, states), BF16), jax.ShapeDtypeStruct((count, length, states), F32)]
        + [jax.ShapeDtypeStruct((count, length, states), BF16)] * 3,
        in_specs=[SMEM, SMEM] + [VMEM] * 5,
        out_specs=[VMEM] * 5,
        scratch_shapes=[pltpu.VMEM((width, states), F32), pltpu.VMEM((SPAN, count, length, states), F32)],
        compiler_params=pltpu.CompilerParams(vmem_limit_bytes=32 * 2**20),
        cost_estimate=pl.CostEstimate(flops=2 * 10**9, bytes_accessed=8 * 2**20, transcendentals=0),
        name="owner_state",
    )(rank, resp_prefix, state, *carried)


def sum_kernel(back0, back1, back2, back3, g_keys, g_values, g_tail):
    rows = g_keys.shape[1]
    for half, out in enumerate((g_keys, g_values)):
        total = back0[half]
        for back in (back1, back2, back3):
            total = total + back[half].astype(F32)
        out[0] = total[0:rows]
        for part in range(2):
            lo = half * 1024 + part * 512
            g_tail[0, :, lo : lo + 512] = total[rows + 8 * part : rows + 8 * part + 3]


def sum_back(backs, tail_shape):
    rows = backs[0].shape[1] - 16
    width = backs[0].shape[2]
    return pl.pallas_call(
        sum_kernel,
        out_shape=[
            jax.ShapeDtypeStruct((1, rows, width), F32),
            jax.ShapeDtypeStruct((1, rows, width), F32),
            jax.ShapeDtypeStruct(tail_shape, F32),
        ],
        in_specs=[VMEM] * 4,
        out_specs=[VMEM] * 3,
        name="sum_prefix",
    )(*backs)


def all_sum(value):
    length = lax.axis_size("dp")
    if length & (length - 1):
        return lax.psum(value, "dp")
    by = 1
    while by < length:
        value = value + lax.ppermute(value, "dp", [(i, i ^ by) for i in range(length)])
        by *= 2
    return value


def on_device(
    token_inputs,
    state_in,
    state_out,
    log_decay,
    skip_gain,
    conv_weight,
    out_cotangent,
    queries,
    own_keys,
    own_values,
    attn_cotangent,
    resp_length,
    resp_prefix,
    prefix_state,
    prefix_tail,
    prefix_keys,
    prefix_values,
    prefix_length,
):
    devices = lax.axis_size("dp")
    rank = lax.axis_index("dp").astype(jnp.int32).reshape(1)
    count, length, _ = token_inputs.shape
    states = state_out.shape[3]
    write = state_in.reshape(count, length, states)
    read = state_out.reshape(count, length, states)
    state = prefix_state.reshape(-1, states)

    decay = jnp.swapaxes(log_decay, 1, 2)
    carries = gather(carry(resp_length, decay, out_cotangent, read), -1)
    tails = [prefix_tail] + [shift(prefix_tail, by) for by in range(1, SPAN)]
    packs = gather(pack(prefix_keys, prefix_values), 1)
    g_inputs, g_tail, g_conv, g_read = mamba(
        rank, resp_prefix, resp_length, skip_gain, token_inputs, tails, conv_weight, write, read, decay, out_cotangent, devices
    )
    g_queries, *backs = attention(
        rank, resp_prefix, resp_length, prefix_length, queries, attn_cotangent, own_keys, own_values, packs, g_tail, devices
    )
    backs = [backs[0]] + [shift(backs[by], -by) for by in range(1, SPAN)]
    g_state, *reads = owner(rank, resp_prefix, state, carries, devices)
    for by in range(SPAN):
        g_read = g_read + (reads[by] if by == 0 else shift(reads[by], by).astype(F32))
    g_prefix_keys, g_prefix_values, g_prefix_tail = sum_back(backs, prefix_tail.shape)
    token_total = count * length * devices
    grad_conv = all_sum(g_conv) * (1.0 / math.sqrt(token_total))
    return (
        g_inputs,
        g_read.astype(BF16).reshape(state_out.shape),
        g_queries,
        g_state.reshape(prefix_state.shape),
        g_prefix_tail,
        g_prefix_keys,
        g_prefix_values,
        grad_conv,
    )


def solution(mesh):
    split = ("groups", "dp")
    placed = (
        P(split, None, None),
        P(split, None, None, None),
        P(split, None, None, None),
        P(split, None, None),
        P(),
        P(),
        P(split, None, None),
        P(split, None, None),
        P(split, None, None),
        P(split, None, None),
        P(split, None, None),
        P(split),
        P("groups"),
        P(split, None, None, None),
        P(split, None, None),
        P(split, None, None),
        P(split, None, None),
        P("groups"),
    )
    return jax.shard_map(
        on_device,
        mesh=mesh,
        in_specs=placed,
        out_specs=(
            P(split, None, None),
            P(split, None, None, None),
            P(split, None, None),
            P(split, None, None, None),
            P(split, None, None),
            P(split, None, None),
            P(split, None, None),
            P("groups", None),
        ),
        check_vma=False,
    )
```

```python
import functools
import math

import jax
import jax.numpy as jnp
from jax import lax
from jax.experimental import pallas as pl
from jax.experimental.pallas import tpu as pltpu
from jax.sharding import PartitionSpec as P

ATT_HEADS = 32
KV_HEADS = 4
ATT_DIM = 128
HEADS = 32
HEAD_DIM = 64
SPAN = 4
REPEAT = ATT_HEADS // KV_HEADS
NEG_FILL = -1e30
F32 = jnp.float32
BF16 = jnp.bfloat16

SMEM = pl.BlockSpec(memory_space=pltpu.SMEM)
VMEM = pl.BlockSpec(memory_space=pltpu.VMEM)


def shift(value, by):
    length = lax.axis_size("dp")
    return lax.ppermute(value, "dp", [(i, (i + by) % length) for i in range(length)])


def nt(a, b):
    return lax.dot_general(a, b, (((1,), (1,)), ((), ())), preferred_element_type=F32)


def tn(a, b):
    return lax.dot_general(a, b, (((0,), (0,)), ((), ())), preferred_element_type=F32)


def nn(a, b):
    return lax.dot_general(a, b, (((1,), (0,)), ((), ())), preferred_element_type=F32)


def pack_kernel(keys, values, tail, out, rows8):
    rows = keys.shape[1]
    out[0, 0:rows, :] = keys[0]
    out[1, 0:rows, :] = values[0]
    rows8[...] = jnp.zeros_like(rows8)
    rows8[5:8, :] = tail[0].astype(F32)
    for half in range(2):
        upper = rows8[:, half * 1024 : half * 1024 + 512]
        lower = rows8[:, half * 1024 + 512 : half * 1024 + 1024]
        out[half, rows : rows + 16, :] = jnp.concatenate([upper, lower], axis=0).astype(BF16)


def pack(prefix_keys, prefix_values, prefix_tail):
    rows, width = prefix_keys.shape[1:]
    return pl.pallas_call(
        pack_kernel,
        out_shape=jax.ShapeDtypeStruct((2, rows + 16, width), BF16),
        in_specs=[VMEM] * 3,
        out_specs=VMEM,
        scratch_shapes=[pltpu.VMEM((8, prefix_tail.shape[2]), F32)],
        name="pack_prefix",
    )(prefix_keys, prefix_values, prefix_tail)


def running_sum(log_decay):
    heads, length = log_decay.shape
    row = lax.broadcasted_iota(jnp.int32, (length, length), 0)
    col = lax.broadcasted_iota(jnp.int32, (length, length), 1)
    upper = (row <= col).astype(F32)
    rows = lax.dot_general(
        log_decay,
        upper,
        (((1,), (0,)), ((), ())),
        precision=lax.Precision.HIGHEST,
        preferred_element_type=F32,
    )
    return jnp.concatenate([rows, jnp.zeros((128 - heads, length), F32)], axis=0).T, rows


def carry_kernel(resp_length, log_decay, cotangent, read, out):
    length = cotangent.shape[1]
    width = cotangent.shape[2]
    live_to = resp_length[pl.program_id(0)]
    raised = jnp.exp(running_sum(log_decay[0])[0])
    live = lax.broadcasted_iota(jnp.int32, (length, 2 * HEAD_DIM), 0) < live_to
    first = lax.broadcasted_iota(jnp.int32, (length, 2 * HEAD_DIM), 1) < HEAD_DIM
    for pair in range(width // (2 * HEAD_DIM)):
        lanes = slice(pair * 2 * HEAD_DIM, (pair + 1) * 2 * HEAD_DIM)
        factor = jnp.where(first, raised[:, 2 * pair : 2 * pair + 1], raised[:, 2 * pair + 1 : 2 * pair + 2])
        factor = jnp.where(live, factor, 0.0)
        out[0, :, lanes] = (factor * cotangent[0, :, lanes].astype(F32)).astype(BF16)
    out[0, :, width:] = read[0]


def carry(resp_length, log_decay, out_cotangent, state_out):
    count, length, width = out_cotangent.shape
    heads = log_decay.shape[1]
    states = state_out.shape[2]
    return pl.pallas_call(
        carry_kernel,
        grid=(count,),
        out_shape=jax.ShapeDtypeStruct((count, length, width + states), BF16),
        in_specs=[
            SMEM,
            pl.BlockSpec((1, heads, length), lambda r: (r, 0, 0)),
            pl.BlockSpec((1, length, width), lambda r: (r, 0, 0)),
            pl.BlockSpec((1, length, states), lambda r: (r, 0, 0)),
        ],
        out_specs=pl.BlockSpec((1, length, width + states), lambda r: (r, 0, 0)),
        name="carry_cotangent",
    )(resp_length, log_decay, out_cotangent, state_out)


def relayed(rank):
    even = rank % 2 == 0
    return 0, 2, jnp.where(even, 1, 3), jnp.where(even, 3, 1)


def swap(value, by):
    return lax.ppermute(value, "dp", [(i, i ^ by) for i in range(lax.axis_size("dp"))])


def two_and_last(value, sign):
    length = lax.axis_size("dp")
    if sign > 0:
        pairs = [(i, (i + (3 if i % 2 else 1)) % length) for i in range(length)]
    else:
        pairs = [(i, (i - (1 if i % 2 else 3)) % length) for i in range(length)]
    return shift(value, 2 * sign), lax.ppermute(value, "dp", pairs)


def after(value, *others):
    return lax.optimization_barrier((value,) + others)[0]


def distance_to(rank, owner, devices):
    gap = rank - owner
    return jnp.where(gap < 0, gap + devices, gap)


def mamba_kernel(
    devices,
    rank_ref,
    resp_prefix,
    resp_length,
    skip_gain,
    inputs,
    pack0,
    pack1,
    pack2,
    pack3,
    conv_weight,
    write,
    read,
    log_decay,
    cotangent,
    g_inputs,
    g_tail,
    g_conv,
    g_read,
    padded,
    shifted,
    inner,
):
    resp = pl.program_id(0)
    length = inputs.shape[1]
    width = inputs.shape[2]
    taps = conv_weight.shape[0]
    rank = rank_ref[0]
    live_to = resp_length[resp]
    gap = distance_to(rank, resp_prefix[2 * rank + resp], devices)
    for step, packed in zip(relayed(rank), (pack0, pack1, pack2, pack3)):

        @pl.when(gap == step)
        def _(packed=packed):
            for half in range(2):
                rows = packed[half].astype(F32)
                for part in range(2):
                    lo = half * 1024 + part * 512
                    padded[0:8, lo : lo + 512] = rows[8 * part : 8 * part + 8]

    padded[8 : 8 + length, :] = inputs[0].astype(F32)
    decay_sum, decay_rows = running_sum(log_decay[0])
    s_index = lax.broadcasted_iota(jnp.int32, (length, length), 0)
    t_index = lax.broadcasted_iota(jnp.int32, (length, length), 1)
    causal = s_index <= t_index
    mixing = nt(write[0], read[0])
    live = lax.broadcasted_iota(jnp.int32, (length, 2 * HEAD_DIM), 0) < live_to
    first = lax.broadcasted_iota(jnp.int32, (length, 2 * HEAD_DIM), 1) < HEAD_DIM
    inner[...] = jnp.zeros_like(inner)
    for pair in range(width // (2 * HEAD_DIM)):
        lo = pair * 2 * HEAD_DIM
        lanes = slice(lo, lo + 2 * HEAD_DIM)
        weight = [conv_weight[k : k + 1, lanes] for k in range(taps)]
        mixed = weight[0] * padded[5 : 5 + length, lanes]
        for k in range(1, taps):
            mixed = mixed + weight[k] * padded[5 + k : 5 + k + length, lanes]
        gate = jax.nn.sigmoid(mixed)
        activated = (mixed * gate).astype(BF16)
        d_out = jnp.where(live, cotangent[0, :, lanes].astype(F32), 0.0)
        both = jnp.concatenate(
            [jnp.where(first, d_out, 0.0).astype(BF16), jnp.where(first, 0.0, d_out).astype(BF16)], axis=0
        )
        d_weights = nt(activated, both)
        decays = []
        for head in (2 * pair, 2 * pair + 1):
            lag = decay_rows[head : head + 1, :] - decay_sum[:, head : head + 1]
            decays.append(jnp.exp(jnp.where(causal, lag, NEG_FILL)))
        weights = jnp.concatenate([(d * mixing).astype(BF16) for d in decays], axis=1)
        inner[...] += decays[0] * d_weights[:, :length] + decays[1] * d_weights[:, length:]
        gain = jnp.where(first[0:1], skip_gain[2 * pair], skip_gain[2 * pair + 1])
        d_act = nn(weights, both) + gain * d_out
        d_mixed = d_act * (gate * (1.0 + mixed * (1.0 - gate)))
        shifted[0:8, lanes] = jnp.zeros((8, 2 * HEAD_DIM), F32)
        shifted[8 : 8 + length, lanes] = d_mixed
        shifted[8 + length : 16 + length, lanes] = jnp.zeros((8, 2 * HEAD_DIM), F32)
        total = weight[0] * shifted[11 : 11 + length, lanes]
        early = weight[0] * shifted[8:16, lanes]
        for k in range(1, taps):
            total = total + weight[k] * shifted[11 - k : 11 - k + length, lanes]
            early = early + weight[k] * shifted[8 - k : 16 - k, lanes]
        g_inputs[0, :, lanes] = total.astype(BF16)
        g_tail[0, lo // 512, :, lo % 512 : lo % 512 + 2 * HEAD_DIM] = early
        rows = [
            jnp.sum(d_mixed * padded[5 + k : 5 + k + length, lanes], axis=0, keepdims=True) for k in range(taps)
        ]
        rows = jnp.concatenate(rows, axis=0)

        @pl.when(resp == 0)
        def _(rows=rows, lanes=lanes):
            g_conv[:, lanes] = rows

        @pl.when(resp > 0)
        def _(rows=rows, lanes=lanes):
            g_conv[:, lanes] += rows

    g_read[0] = tn(inner[...].astype(BF16), write[0])


def mamba(rank, resp_prefix, resp_length, skip_gain, inputs, packs, conv_weight, write, read, log_decay, cotangent, devices):
    count, length, width = inputs.shape
    heads = log_decay.shape[1]
    states = read.shape[2]
    taps = conv_weight.shape[0]
    whole = pl.BlockSpec((2, 16, packs[0].shape[2]), lambda r: (0, (packs[0].shape[1] - 16) // 16, 0))
    return pl.pallas_call(
        functools.partial(mamba_kernel, devices),
        grid=(count,),
        out_shape=[
            jax.ShapeDtypeStruct((count, length, width), BF16),
            jax.ShapeDtypeStruct((count, 4, 8, 512), F32),
            jax.ShapeDtypeStruct((taps, width), F32),
            jax.ShapeDtypeStruct((count, length, states), F32),
        ],
        in_specs=[
            SMEM,
            SMEM,
            SMEM,
            SMEM,
            pl.BlockSpec((1, length, width), lambda r: (r, 0, 0)),
            whole,
            whole,
            whole,
            whole,
            pl.BlockSpec((taps, width), lambda r: (0, 0)),
            pl.BlockSpec((1, length, states), lambda r: (r, 0, 0)),
            pl.BlockSpec((1, length, states), lambda r: (r, 0, 0)),
            pl.BlockSpec((1, heads, length), lambda r: (r, 0, 0)),
            pl.BlockSpec((1, length, width), lambda r: (r, 0, 0)),
        ],
        out_specs=[
            pl.BlockSpec((1, length, width), lambda r: (r, 0, 0)),
            pl.BlockSpec((1, 4, 8, 512), lambda r: (r, 0, 0, 0)),
            pl.BlockSpec((taps, width), lambda r: (0, 0)),
            pl.BlockSpec((1, length, states), lambda r: (r, 0, 0)),
        ],
        scratch_shapes=[
            pltpu.VMEM((length + 8, width), F32),
            pltpu.VMEM((length + 16, width), F32),
            pltpu.VMEM((length, length), F32),
        ],
        compiler_params=pltpu.CompilerParams(vmem_limit_bytes=32 * 2**20),
        cost_estimate=pl.CostEstimate(flops=2 * 10**9, bytes_accessed=8 * 2**20, transcendentals=10**6),
        name="mamba_grads",
    )(rank, resp_prefix, resp_length, skip_gain, inputs, *packs, conv_weight, write, read, log_decay, cotangent)


def attention_kernel(
    devices,
    rank_ref,
    resp_prefix,
    resp_length,
    prefix_length,
    queries,
    cotangent,
    own_keys,
    own_values,
    pack0,
    pack1,
    pack2,
    pack3,
    g_tail,
    g_queries,
    back0,
    back1,
    back2,
    back3,
    keys,
    values,
    kept,
):
    resp = pl.program_id(1)
    length = queries.shape[1]
    rows = keys.shape[0] - length
    rank = rank_ref[0]
    prefix = resp_prefix[2 * rank + resp]
    pref_len = prefix_length[prefix]
    live_to = resp_length[resp]
    scale = 1.0 / math.sqrt(ATT_DIM)
    gap = distance_to(rank, prefix, devices)
    for step, packed in zip(relayed(rank), (pack0, pack1, pack2, pack3)):

        @pl.when(gap == step)
        def _(packed=packed):
            keys[0:rows, :] = packed[0, 0:rows, :]
            values[0:rows, :] = packed[1, 0:rows, :]

    keys[rows : rows + length, :] = own_keys[0]
    values[rows : rows + length, :] = own_values[0]
    j_index = lax.broadcasted_iota(jnp.int32, (rows + length, 2 * length), 0)
    t_index = lax.broadcasted_iota(jnp.int32, (rows + length, 2 * length), 1)
    t_index = jnp.where(t_index >= length, t_index - length, t_index)
    bound = jnp.where(j_index < rows, pref_len, t_index + rows + 1)
    bias = jnp.where(j_index < bound, 0.0, NEG_FILL)
    live = lax.broadcasted_iota(jnp.int32, (length, ATT_DIM), 0) < live_to
    all_keys = keys[...]
    all_values = values[...]
    g_keys = jnp.zeros((rows, ATT_DIM), F32)
    g_values = jnp.zeros((rows, ATT_DIM), F32)
    for duo in range(REPEAT // 2):
        spans = [slice((2 * duo + i) * ATT_DIM, (2 * duo + i + 1) * ATT_DIM) for i in range(2)]
        query = jnp.concatenate([queries[0, :, span] for span in spans], axis=0)
        d_out = jnp.concatenate(
            [jnp.where(live, cotangent[0, :, span].astype(F32), 0.0).astype(BF16) for span in spans], axis=0
        )
        scores = nt(all_keys, query) * scale + bias
        top = jnp.max(scores, axis=0, keepdims=True)
        raised = jnp.exp(scores - top)
        probs = raised * (1.0 / jnp.sum(raised, axis=0, keepdims=True))
        probs_low = probs.astype(BF16)
        d_probs = nt(all_values, d_out)
        delta = jnp.sum(probs_low.astype(F32) * d_probs, axis=0, keepdims=True)
        d_scores = (probs * ((d_probs - delta) * scale)).astype(BF16)
        g_query = tn(d_scores, all_keys)
        for i, span in enumerate(spans):
            g_queries[0, :, span] = g_query[i * length : (i + 1) * length].astype(BF16)
        g_keys = g_keys + nn(d_scores[0:rows], query)
        g_values = g_values + nn(probs_low[0:rows], d_out)

    @pl.when(resp == 0)
    def _():
        kept[0] = g_keys
        kept[1] = g_values

    @pl.when(resp == 1)
    def _():
        before = distance_to(rank, resp_prefix[2 * rank], devices)
        for step, back in enumerate((back0, back1, back2, back3)):
            one = jnp.where(before == step, 1.0, 0.0)
            two = jnp.where(gap == step, 1.0, 0.0)
            back[0, 0:rows, :] = (kept[0] * one + g_keys * two).astype(back.dtype)
            back[1, 0:rows, :] = (kept[1] * one + g_values * two).astype(back.dtype)
            for half in range(2):
                upper = g_tail[0, 2 * half] * one + g_tail[1, 2 * half] * two
                lower = g_tail[0, 2 * half + 1] * one + g_tail[1, 2 * half + 1] * two
                back[half, rows : rows + 16, :] = jnp.concatenate([upper, lower], axis=0).astype(back.dtype)


def attention(rank, resp_prefix, resp_length, prefix_length, queries, cotangent, own_keys, own_values, packs, g_tail, devices):
    count, length, width = queries.shape
    rows = packs[0].shape[1] - 16
    group = REPEAT * ATT_DIM
    packed = pl.BlockSpec((2, rows, ATT_DIM), lambda h, r: (0, 0, h))
    back_block = pl.BlockSpec((2, rows + 16, ATT_DIM), lambda h, r: (0, 0, h))
    back = (2, rows + 16, KV_HEADS * ATT_DIM)
    return pl.pallas_call(
        functools.partial(attention_kernel, devices),
        grid=(KV_HEADS, count),
        out_shape=[
            jax.ShapeDtypeStruct((count, length, width), BF16),
            jax.ShapeDtypeStruct(back, F32),
            jax.ShapeDtypeStruct(back, BF16),
            jax.ShapeDtypeStruct(back, BF16),
            jax.ShapeDtypeStruct(back, BF16),
        ],
        in_specs=[
            SMEM,
            SMEM,
            SMEM,
            SMEM,
            pl.BlockSpec((1, length, group), lambda h, r: (r, 0, h)),
            pl.BlockSpec((1, length, group), lambda h, r: (r, 0, h)),
            pl.BlockSpec((1, length, ATT_DIM), lambda h, r: (r, 0, h)),
            pl.BlockSpec((1, length, ATT_DIM), lambda h, r: (r, 0, h)),
            packed,
            packed,
            packed,
            packed,
            pl.BlockSpec((count, 4, 8, ATT_DIM), lambda h, r: (0, 0, 0, h)),
        ],
        out_specs=[
            pl.BlockSpec((1, length, group), lambda h, r: (r, 0, h)),
            back_block,
            back_block,
            back_block,
            back_block,
        ],
        scratch_shapes=[
            pltpu.VMEM((rows + length, ATT_DIM), BF16),
            pltpu.VMEM((rows + length, ATT_DIM), BF16),
            pltpu.VMEM((2, rows, ATT_DIM), F32),
        ],
        compiler_params=pltpu.CompilerParams(vmem_limit_bytes=32 * 2**20),
        cost_estimate=pl.CostEstimate(flops=4 * 10**9, bytes_accessed=8 * 2**20, transcendentals=2 * 10**6),
        name="attention_grads",
    )(rank, resp_prefix, resp_length, prefix_length, queries, cotangent, own_keys, own_values, *packs, g_tail)


def owner_kernel(devices, rank_ref, resp_prefix, state, car0, car1, car2, car3, g_state, dr0, dr1, dr2, dr3, total, parts):
    rank = rank_ref[0]
    even = rank % 2 == 0
    width = state.shape[0]
    chunk = 512
    total[...] = jnp.zeros_like(total)
    for slot, (step, carried) in enumerate(
        zip((0, 2, jnp.where(even, 3, 1), jnp.where(even, 1, 3)), (car0, car1, car2, car3))
    ):
        sender = rank + step
        sender = jnp.where(sender >= devices, sender - devices, sender)
        for resp in range(2):
            mine = resp_prefix[2 * sender + resp] == rank

            @pl.when(mine)
            def _(carried=carried, slot=slot, resp=resp):
                read = carried[resp, :, width:]
                acc = None
                for at in range(0, width, chunk):
                    piece = carried[resp, :, at : at + chunk]
                    term = nn(piece, state[at : at + chunk, :])
                    acc = term if acc is None else acc + term
                    total[at : at + chunk, :] += tn(piece, read)
                parts[slot, resp] = acc

            @pl.when(jnp.logical_not(mine))
            def _(slot=slot, resp=resp):
                parts[slot, resp] = jnp.zeros(parts.shape[2:], F32)

    g_state[...] = total[...].astype(BF16)
    dr0[...] = parts[0]
    dr2[...] = parts[1].astype(BF16)

    @pl.when(even)
    def _():
        dr3[...] = parts[2].astype(BF16)
        dr1[...] = parts[3].astype(BF16)

    @pl.when(jnp.logical_not(even))
    def _():
        dr1[...] = parts[2].astype(BF16)
        dr3[...] = parts[3].astype(BF16)


def owner(rank, resp_prefix, state, carried, devices):
    width, states = state.shape
    count, length = carried[0].shape[:2]
    return pl.pallas_call(
        functools.partial(owner_kernel, devices),
        out_shape=[jax.ShapeDtypeStruct((width, states), BF16), jax.ShapeDtypeStruct((count, length, states), F32)]
        + [jax.ShapeDtypeStruct((count, length, states), BF16)] * 3,
        in_specs=[SMEM, SMEM] + [VMEM] * 5,
        out_specs=[VMEM] * 5,
        scratch_shapes=[pltpu.VMEM((width, states), F32), pltpu.VMEM((SPAN, count, length, states), F32)],
        compiler_params=pltpu.CompilerParams(vmem_limit_bytes=32 * 2**20),
        cost_estimate=pl.CostEstimate(flops=2 * 10**9, bytes_accessed=8 * 2**20, transcendentals=0),
        name="owner_state",
    )(rank, resp_prefix, state, *carried)


def sum_kernel(back0, back1, back2, back3, g_keys, g_values, g_tail):
    rows = g_keys.shape[1]
    for half, out in enumerate((g_keys, g_values)):
        total = back0[half]
        for back in (back1, back2, back3):
            total = total + back[half].astype(F32)
        out[0] = total[0:rows]
        for part in range(2):
            lo = half * 1024 + part * 512
            g_tail[:, 0, lo : lo + 512] = total[rows + 8 * part : rows + 8 * part + 3]


def sum_back(backs, tail_shape):
    rows = backs[0].shape[1] - 16
    width = backs[0].shape[2]
    return pl.pallas_call(
        sum_kernel,
        out_shape=[
            jax.ShapeDtypeStruct((1, rows, width), F32),
            jax.ShapeDtypeStruct((1, rows, width), F32),
            jax.ShapeDtypeStruct((tail_shape[1], 1, tail_shape[2]), F32),
        ],
        in_specs=[VMEM] * 4,
        out_specs=[VMEM] * 3,
        name="sum_prefix",
    )(*backs)


def on_device(
    token_inputs,
    state_in,
    state_out,
    log_decay,
    skip_gain,
    conv_weight,
    out_cotangent,
    queries,
    own_keys,
    own_values,
    attn_cotangent,
    resp_length,
    resp_prefix,
    prefix_state,
    prefix_tail,
    prefix_keys,
    prefix_values,
    prefix_length,
):
    devices = lax.axis_size("dp")
    rank = lax.axis_index("dp").astype(jnp.int32).reshape(1)
    count, length, _ = token_inputs.shape
    states = state_out.shape[3]
    write = state_in.reshape(count, length, states)
    read = state_out.reshape(count, length, states)
    state = prefix_state.reshape(-1, states)

    decay = jnp.swapaxes(log_decay, 1, 2)
    packed = pack(prefix_keys, prefix_values, prefix_tail)
    pack_two, pack_last = two_and_last(packed, 1)
    carried = carry(after(resp_length, packed), decay, out_cotangent, read)
    pack_two, pack_last, carried = lax.optimization_barrier((pack_two, pack_last, carried))
    carry_two, carry_last = two_and_last(carried, -1)
    pack_relay = swap(pack_two, 1)
    packs = [packed, pack_two, pack_relay, pack_last]
    g_inputs, g_tail, g_conv, g_read = mamba(
        rank, resp_prefix, resp_length, skip_gain, token_inputs, packs, conv_weight, write, read, decay, out_cotangent, devices
    )
    conv = g_conv + swap(g_conv, 1)
    g_queries, *backs = attention(
        rank, resp_prefix, after(resp_length, carry_last), prefix_length, queries, attn_cotangent, own_keys, own_values, packs, g_tail, devices
    )
    carry_two = after(carry_two, backs[1])
    carry_relay = swap(carry_two, 1)
    conv = after(conv, carry_two)
    conv = conv + swap(conv, 2)
    backs = [backs[0]] + [shift(backs[by], -by) for by in range(1, SPAN)]
    g_state, *reads = owner(rank, resp_prefix, state, [carried, carry_two, carry_relay, carry_last], devices)
    by = 4
    while by < devices:
        conv = conv + (swap(conv, by) if devices & (devices - 1) == 0 else 0)
        by *= 2
    for by in range(SPAN):
        g_read = g_read + (reads[by] if by == 0 else shift(reads[by], by).astype(F32))
    g_prefix_keys, g_prefix_values, g_prefix_tail = sum_back(backs, prefix_tail.shape)
    token_total = count * length * devices
    grad_conv = conv * (1.0 / math.sqrt(token_total))
    return (
        g_inputs,
        g_read.astype(BF16).reshape(state_out.shape),
        g_queries,
        g_state.reshape(prefix_state.shape),
        jnp.swapaxes(g_prefix_tail, 0, 1),
        g_prefix_keys,
        g_prefix_values,
        grad_conv,
    )


def solution(mesh):
    split = ("groups", "dp")
    placed = (
        P(split, None, None),
        P(split, None, None, None),
        P(split, None, None, None),
        P(split, None, None),
        P(),
        P(),
        P(split, None, None),
        P(split, None, None),
        P(split, None, None),
        P(split, None, None),
        P(split, None, None),
        P(split),
        P("groups"),
        P(split, None, None, None),
        P(split, None, None),
        P(split, None, None),
        P(split, None, None),
        P("groups"),
    )
    return jax.shard_map(
        on_device,
        mesh=mesh,
        in_specs=placed,
        out_specs=(
            P(split, None, None),
            P(split, None, None, None),
            P(split, None, None),
            P(split, None, None, None),
            P(split, None, None),
            P(split, None, None),
            P(split, None, None),
            P("groups", None),
        ),
        check_vma=False,
    )
```

```python
import functools
import math

import jax
import jax.numpy as jnp
from jax import lax
from jax.experimental import pallas as pl
from jax.experimental.pallas import tpu as pltpu
from jax.sharding import PartitionSpec as P

ATT_HEADS = 32
KV_HEADS = 4
ATT_DIM = 128
HEADS = 32
HEAD_DIM = 64
SPAN = 4
REPEAT = ATT_HEADS // KV_HEADS
NEG_FILL = -1e30
F32 = jnp.float32
BF16 = jnp.bfloat16

SMEM = pl.BlockSpec(memory_space=pltpu.SMEM)
VMEM = pl.BlockSpec(memory_space=pltpu.VMEM)


def shift(value, by):
    length = lax.axis_size("dp")
    return lax.ppermute(value, "dp", [(i, (i + by) % length) for i in range(length)])


def nt(a, b):
    return lax.dot_general(a, b, (((1,), (1,)), ((), ())), preferred_element_type=F32)


def tn(a, b):
    return lax.dot_general(a, b, (((0,), (0,)), ((), ())), preferred_element_type=F32)


def nn(a, b):
    return lax.dot_general(a, b, (((1,), (0,)), ((), ())), preferred_element_type=F32)


def pack_kernel(keys, values, out):
    out[0] = keys[0]
    out[1] = values[0]


def pack(prefix_keys, prefix_values):
    return pl.pallas_call(
        pack_kernel,
        out_shape=jax.ShapeDtypeStruct((2,) + prefix_keys.shape[1:], BF16),
        in_specs=[VMEM] * 2,
        out_specs=VMEM,
        name="pack_prefix",
    )(prefix_keys, prefix_values)


def running_sum(log_decay):
    heads, length = log_decay.shape
    row = lax.broadcasted_iota(jnp.int32, (length, length), 0)
    col = lax.broadcasted_iota(jnp.int32, (length, length), 1)
    upper = (row <= col).astype(F32)
    rows = lax.dot_general(
        log_decay,
        upper,
        (((1,), (0,)), ((), ())),
        precision=lax.Precision.HIGHEST,
        preferred_element_type=F32,
    )
    return jnp.concatenate([rows, jnp.zeros((128 - heads, length), F32)], axis=0).T, rows


def carry_kernel(resp_length, log_decay, cotangent, read, out):
    length = cotangent.shape[1]
    width = cotangent.shape[2]
    live_to = resp_length[pl.program_id(0)]
    raised = jnp.exp(running_sum(log_decay[0])[0])
    live = lax.broadcasted_iota(jnp.int32, (length, 2 * HEAD_DIM), 0) < live_to
    first = lax.broadcasted_iota(jnp.int32, (length, 2 * HEAD_DIM), 1) < HEAD_DIM
    for pair in range(width // (2 * HEAD_DIM)):
        lanes = slice(pair * 2 * HEAD_DIM, (pair + 1) * 2 * HEAD_DIM)
        factor = jnp.where(first, raised[:, 2 * pair : 2 * pair + 1], raised[:, 2 * pair + 1 : 2 * pair + 2])
        factor = jnp.where(live, factor, 0.0)
        out[0, :, lanes] = (factor * cotangent[0, :, lanes].astype(F32)).astype(BF16)
    out[0, :, width:] = read[0]


def carry(resp_length, log_decay, out_cotangent, state_out):
    count, length, width = out_cotangent.shape
    heads = log_decay.shape[1]
    states = state_out.shape[2]
    return pl.pallas_call(
        carry_kernel,
        grid=(count,),
        out_shape=jax.ShapeDtypeStruct((count, length, width + states), BF16),
        in_specs=[
            SMEM,
            pl.BlockSpec((1, heads, length), lambda r: (r, 0, 0)),
            pl.BlockSpec((1, length, width), lambda r: (r, 0, 0)),
            pl.BlockSpec((1, length, states), lambda r: (r, 0, 0)),
        ],
        out_specs=pl.BlockSpec((1, length, width + states), lambda r: (r, 0, 0)),
        name="carry_cotangent",
    )(resp_length, log_decay, out_cotangent, state_out)


def swap(value, by):
    return lax.ppermute(value, "dp", [(i, i ^ by) for i in range(lax.axis_size("dp"))])


def after(value, *others):
    return lax.optimization_barrier((value,) + others)[0]


def distance_to(rank, owner, devices):
    gap = rank - owner
    return jnp.where(gap < 0, gap + devices, gap)


def mamba_kernel(
    devices,
    rank_ref,
    resp_prefix,
    resp_length,
    skip_gain,
    inputs,
    tail0,
    tail1,
    tail2,
    tail3,
    conv_weight,
    write,
    read,
    log_decay,
    cotangent,
    g_inputs,
    g_tail,
    g_conv,
    g_read,
    padded,
    shifted,
    inner,
):
    resp = pl.program_id(0)
    length = inputs.shape[1]
    width = inputs.shape[2]
    taps = conv_weight.shape[0]
    rank = rank_ref[0]
    live_to = resp_length[resp]
    gap = distance_to(rank, resp_prefix[2 * rank + resp], devices)
    for step, tail in enumerate((tail0, tail1, tail2, tail3)):

        @pl.when(gap == step)
        def _(tail=tail):
            padded[5:8, :] = tail[0].astype(F32)

    padded[8 : 8 + length, :] = inputs[0].astype(F32)
    decay_sum, decay_rows = running_sum(log_decay[0])
    s_index = lax.broadcasted_iota(jnp.int32, (length, length), 0)
    t_index = lax.broadcasted_iota(jnp.int32, (length, length), 1)
    causal = s_index <= t_index
    mixing = nt(write[0], read[0])
    live = lax.broadcasted_iota(jnp.int32, (length, 2 * HEAD_DIM), 0) < live_to
    first = lax.broadcasted_iota(jnp.int32, (length, 2 * HEAD_DIM), 1) < HEAD_DIM
    inner[...] = jnp.zeros_like(inner)
    for pair in range(width // (2 * HEAD_DIM)):
        lo = pair * 2 * HEAD_DIM
        lanes = slice(lo, lo + 2 * HEAD_DIM)
        weight = [conv_weight[k : k + 1, lanes] for k in range(taps)]
        mixed = weight[0] * padded[5 : 5 + length, lanes]
        for k in range(1, taps):
            mixed = mixed + weight[k] * padded[5 + k : 5 + k + length, lanes]
        gate = jax.nn.sigmoid(mixed)
        activated = (mixed * gate).astype(BF16)
        d_out = jnp.where(live, cotangent[0, :, lanes].astype(F32), 0.0)
        both = jnp.concatenate(
            [jnp.where(first, d_out, 0.0).astype(BF16), jnp.where(first, 0.0, d_out).astype(BF16)], axis=0
        )
        d_weights = nt(activated, both)
        decays = []
        for head in (2 * pair, 2 * pair + 1):
            lag = decay_rows[head : head + 1, :] - decay_sum[:, head : head + 1]
            decays.append(jnp.exp(jnp.where(causal, lag, NEG_FILL)))
        weights = jnp.concatenate([(d * mixing).astype(BF16) for d in decays], axis=1)
        inner[...] += decays[0] * d_weights[:, :length] + decays[1] * d_weights[:, length:]
        gain = jnp.where(first[0:1], skip_gain[2 * pair], skip_gain[2 * pair + 1])
        d_act = nn(weights, both) + gain * d_out
        d_mixed = d_act * (gate * (1.0 + mixed * (1.0 - gate)))
        shifted[0:8, lanes] = jnp.zeros((8, 2 * HEAD_DIM), F32)
        shifted[8 : 8 + length, lanes] = d_mixed
        shifted[8 + length : 16 + length, lanes] = jnp.zeros((8, 2 * HEAD_DIM), F32)
        total = weight[0] * shifted[11 : 11 + length, lanes]
        early = weight[0] * shifted[8:16, lanes]
        for k in range(1, taps):
            total = total + weight[k] * shifted[11 - k : 11 - k + length, lanes]
            early = early + weight[k] * shifted[8 - k : 16 - k, lanes]
        g_inputs[0, :, lanes] = total.astype(BF16)
        g_tail[0, lo // 512, :, lo % 512 : lo % 512 + 2 * HEAD_DIM] = early
        rows = [
            jnp.sum(d_mixed * padded[5 + k : 5 + k + length, lanes], axis=0, keepdims=True) for k in range(taps)
        ]
        rows = jnp.concatenate(rows, axis=0)


        @pl.when(resp == 0)
        def _(rows=rows, lanes=lanes):
            g_conv[:, lanes] = rows

        @pl.when(resp > 0)
        def _(rows=rows, lanes=lanes):
            g_conv[:, lanes] += rows

    g_read[0] = tn(inner[...].astype(BF16), write[0])


def mamba(rank, resp_prefix, resp_length, skip_gain, inputs, tails, conv_weight, write, read, log_decay, cotangent, devices):
    count, length, width = inputs.shape
    heads = log_decay.shape[1]
    states = read.shape[2]
    taps = conv_weight.shape[0]
    whole = pl.BlockSpec(tails[0].shape, lambda r: (0, 0, 0))
    return pl.pallas_call(
        functools.partial(mamba_kernel, devices),
        grid=(count,),
        out_shape=[
            jax.ShapeDtypeStruct((count, length, width), BF16),
            jax.ShapeDtypeStruct((count, 4, 8, 512), F32),
            jax.ShapeDtypeStruct((taps, width), F32),
            jax.ShapeDtypeStruct((count, length, states), F32),
        ],
        in_specs=[
            SMEM,
            SMEM,
            SMEM,
            SMEM,
            pl.BlockSpec((1, length, width), lambda r: (r, 0, 0)),
            whole,
            whole,
            whole,
            whole,
            pl.BlockSpec((taps, width), lambda r: (0, 0)),
            pl.BlockSpec((1, length, states), lambda r: (r, 0, 0)),
            pl.BlockSpec((1, length, states), lambda r: (r, 0, 0)),
            pl.BlockSpec((1, heads, length), lambda r: (r, 0, 0)),
            pl.BlockSpec((1, length, width), lambda r: (r, 0, 0)),
        ],
        out_specs=[
            pl.BlockSpec((1, length, width), lambda r: (r, 0, 0)),
            pl.BlockSpec((1, 4, 8, 512), lambda r: (r, 0, 0, 0)),
            pl.BlockSpec((taps, width), lambda r: (0, 0)),
            pl.BlockSpec((1, length, states), lambda r: (r, 0, 0)),
        ],
        scratch_shapes=[
            pltpu.VMEM((length + 8, width), F32),
            pltpu.VMEM((length + 16, width), F32),
            pltpu.VMEM((length, length), F32),
        ],
        compiler_params=pltpu.CompilerParams(vmem_limit_bytes=32 * 2**20),
        cost_estimate=pl.CostEstimate(flops=2 * 10**9, bytes_accessed=8 * 2**20, transcendentals=10**6),
        name="mamba_grads",
    )(rank, resp_prefix, resp_length, skip_gain, inputs, *tails, conv_weight, write, read, log_decay, cotangent)


def attention_kernel(
    devices,
    rank_ref,
    resp_prefix,
    resp_length,
    prefix_length,
    queries,
    cotangent,
    own_keys,
    own_values,
    pack0,
    pack1,
    pack2,
    pack3,
    g_tail,
    g_queries,
    back0,
    back1,
    back2,
    back3,
    keys,
    values,
    kept,
):
    resp = pl.program_id(1)
    length = queries.shape[1]
    rows = keys.shape[0] - length
    rank = rank_ref[0]
    prefix = resp_prefix[2 * rank + resp]
    pref_len = prefix_length[prefix]
    live_to = resp_length[resp]
    scale = 1.0 / math.sqrt(ATT_DIM)
    gap = distance_to(rank, prefix, devices)
    for step, packed in enumerate((pack0, pack1, pack2, pack3)):

        @pl.when(gap == step)
        def _(packed=packed):
            keys[0:rows, :] = packed[0, 0:rows, :]
            values[0:rows, :] = packed[1, 0:rows, :]

    keys[rows : rows + length, :] = own_keys[0]
    values[rows : rows + length, :] = own_values[0]
    j_index = lax.broadcasted_iota(jnp.int32, (rows + length, 2 * length), 0)
    t_index = lax.broadcasted_iota(jnp.int32, (rows + length, 2 * length), 1)
    t_index = jnp.where(t_index >= length, t_index - length, t_index)
    bound = jnp.where(j_index < rows, pref_len, t_index + rows + 1)
    bias = jnp.where(j_index < bound, 0.0, NEG_FILL)
    live = lax.broadcasted_iota(jnp.int32, (length, ATT_DIM), 0) < live_to
    all_keys = keys[...]
    all_values = values[...]
    g_keys = jnp.zeros((rows, ATT_DIM), F32)
    g_values = jnp.zeros((rows, ATT_DIM), F32)
    for duo in range(REPEAT // 2):
        spans = [slice((2 * duo + i) * ATT_DIM, (2 * duo + i + 1) * ATT_DIM) for i in range(2)]
        query = jnp.concatenate([queries[0, :, span] for span in spans], axis=0)
        d_out = jnp.concatenate(
            [jnp.where(live, cotangent[0, :, span].astype(F32), 0.0).astype(BF16) for span in spans], axis=0
        )
        scores = nt(all_keys, query) * (scale * math.log2(math.e)) + bias
        top = jnp.max(scores, axis=0, keepdims=True)
        raised = jnp.exp2(scores - top)
        probs = raised * (1.0 / jnp.sum(raised, axis=0, keepdims=True))
        probs_low = probs.astype(BF16)
        d_probs = nt(all_values, d_out)
        delta = jnp.sum(probs * d_probs, axis=0, keepdims=True)
        d_scores = (probs * (d_probs - delta)).astype(BF16)
        g_query = tn(d_scores, all_keys) * scale
        for i, span in enumerate(spans):
            g_queries[0, :, span] = g_query[i * length : (i + 1) * length].astype(BF16)
        g_keys = g_keys + nn(d_scores[0:rows], query)
        g_values = g_values + nn(probs_low[0:rows], d_out)

    g_keys = g_keys * scale

    @pl.when(resp == 0)
    def _():
        kept[0] = g_keys
        kept[1] = g_values

    @pl.when(resp == 1)
    def _():
        before = distance_to(rank, resp_prefix[2 * rank], devices)
        for step, back in enumerate((back0, back1, back2, back3)):
            one = jnp.where(before == step, 1.0, 0.0)
            two = jnp.where(gap == step, 1.0, 0.0)
            back[0, 0:rows, :] = (kept[0] * one + g_keys * two).astype(back.dtype)
            back[1, 0:rows, :] = (kept[1] * one + g_values * two).astype(back.dtype)
            for half in range(2):
                tiles = [g_tail[0, part] * one + g_tail[1, part] * two for part in (2 * half, 2 * half + 1)]
                back[half, rows : rows + 16, :] = jnp.concatenate(tiles, axis=0).astype(back.dtype)


def attention(rank, resp_prefix, resp_length, prefix_length, queries, cotangent, own_keys, own_values, packs, g_tail, devices):
    count, length, width = queries.shape
    rows = packs[0].shape[1]
    group = REPEAT * ATT_DIM
    packed = pl.BlockSpec((2, rows, ATT_DIM), lambda h, r: (0, 0, h))
    back_block = pl.BlockSpec((2, rows + 16, ATT_DIM), lambda h, r: (0, 0, h))
    back = (2, rows + 16, KV_HEADS * ATT_DIM)
    return pl.pallas_call(
        functools.partial(attention_kernel, devices),
        grid=(KV_HEADS, count),
        out_shape=[
            jax.ShapeDtypeStruct((count, length, width), BF16),
            jax.ShapeDtypeStruct(back, F32),
            jax.ShapeDtypeStruct(back, BF16),
            jax.ShapeDtypeStruct(back, BF16),
            jax.ShapeDtypeStruct(back, BF16),
        ],
        in_specs=[
            SMEM,
            SMEM,
            SMEM,
            SMEM,
            pl.BlockSpec((1, length, group), lambda h, r: (r, 0, h)),
            pl.BlockSpec((1, length, group), lambda h, r: (r, 0, h)),
            pl.BlockSpec((1, length, ATT_DIM), lambda h, r: (r, 0, h)),
            pl.BlockSpec((1, length, ATT_DIM), lambda h, r: (r, 0, h)),
            packed,
            packed,
            packed,
            packed,
            pl.BlockSpec((count, 4, 8, ATT_DIM), lambda h, r: (0, 0, 0, h)),
        ],
        out_specs=[
            pl.BlockSpec((1, length, group), lambda h, r: (r, 0, h)),
            back_block,
            back_block,
            back_block,
            back_block,
        ],
        scratch_shapes=[
            pltpu.VMEM((rows + length, ATT_DIM), BF16),
            pltpu.VMEM((rows + length, ATT_DIM), BF16),
            pltpu.VMEM((2, rows, ATT_DIM), F32),
        ],
        compiler_params=pltpu.CompilerParams(vmem_limit_bytes=32 * 2**20),
        cost_estimate=pl.CostEstimate(flops=4 * 10**9, bytes_accessed=8 * 2**20, transcendentals=2 * 10**6),
        name="attention_grads",
    )(rank, resp_prefix, resp_length, prefix_length, queries, cotangent, own_keys, own_values, *packs, g_tail)


def owner_kernel(devices, rank_ref, resp_prefix, state, car0, car1, car2, car3, g_state, dr0, dr1, dr2, dr3, total, parts):
    rank = rank_ref[0]
    even = rank % 2 == 0
    width = state.shape[0]
    chunk = 512
    total[...] = jnp.zeros_like(total)
    for slot, (step, carried) in enumerate(
        zip((0, 2, jnp.where(even, 3, 1), jnp.where(even, 1, 3)), (car0, car1, car2, car3))
    ):
        sender = rank + step
        sender = jnp.where(sender >= devices, sender - devices, sender)
        for resp in range(2):
            mine = resp_prefix[2 * sender + resp] == rank

            @pl.when(mine)
            def _(carried=carried, slot=slot, resp=resp):
                read = carried[resp, :, width:]
                acc = None
                for at in range(0, width, chunk):
                    piece = carried[resp, :, at : at + chunk]
                    term = nn(piece, state[at : at + chunk, :])
                    acc = term if acc is None else acc + term
                    total[at : at + chunk, :] += tn(piece, read)
                parts[slot, resp] = acc

            @pl.when(jnp.logical_not(mine))
            def _(slot=slot, resp=resp):
                parts[slot, resp] = jnp.zeros(parts.shape[2:], F32)

    g_state[...] = total[...].astype(BF16)
    dr0[...] = parts[0]
    dr2[...] = parts[1].astype(BF16)

    @pl.when(even)
    def _():
        dr3[...] = parts[2].astype(BF16)
        dr1[...] = parts[3].astype(BF16)

    @pl.when(jnp.logical_not(even))
    def _():
        dr1[...] = parts[2].astype(BF16)
        dr3[...] = parts[3].astype(BF16)


def owner(rank, resp_prefix, state, carried, devices):
    width, states = state.shape
    count, length = carried[0].shape[:2]
    return pl.pallas_call(
        functools.partial(owner_kernel, devices),
        out_shape=[jax.ShapeDtypeStruct((width, states), BF16), jax.ShapeDtypeStruct((count, length, states), F32)]
        + [jax.ShapeDtypeStruct((count, length, states), BF16)] * 3,
        in_specs=[SMEM, SMEM] + [VMEM] * 5,
        out_specs=[VMEM] * 5,
        scratch_shapes=[pltpu.VMEM((width, states), F32), pltpu.VMEM((SPAN, count, length, states), F32)],
        compiler_params=pltpu.CompilerParams(vmem_limit_bytes=32 * 2**20),
        cost_estimate=pl.CostEstimate(flops=2 * 10**9, bytes_accessed=8 * 2**20, transcendentals=0),
        name="owner_state",
    )(rank, resp_prefix, state, *carried)


def sum_kernel(back0, back1, back2, back3, g_keys, g_values, g_tail):
    rows = g_keys.shape[1]
    for half, out in enumerate((g_keys, g_values)):
        total = back0[half]
        for back in (back1, back2, back3):
            total = total + back[half].astype(F32)
        out[0] = total[0:rows]
        for part in range(2):
            lo = half * 1024 + part * 512
            g_tail[:, 0, lo : lo + 512] = total[rows + 8 * part : rows + 8 * part + 3]


def sum_back(backs, tail_shape):
    rows = backs[0].shape[1] - 16
    width = backs[0].shape[2]
    return pl.pallas_call(
        sum_kernel,
        out_shape=[
            jax.ShapeDtypeStruct((1, rows, width), F32),
            jax.ShapeDtypeStruct((1, rows, width), F32),
            jax.ShapeDtypeStruct((tail_shape[1], 1, tail_shape[2]), F32),
        ],
        in_specs=[VMEM] * 4,
        out_specs=[VMEM] * 3,
        name="sum_prefix",
    )(*backs)


def on_device(
    token_inputs,
    state_in,
    state_out,
    log_decay,
    skip_gain,
    conv_weight,
    out_cotangent,
    queries,
    own_keys,
    own_values,
    attn_cotangent,
    resp_length,
    resp_prefix,
    prefix_state,
    prefix_tail,
    prefix_keys,
    prefix_values,
    prefix_length,
):
    devices = lax.axis_size("dp")
    rank = lax.axis_index("dp").astype(jnp.int32).reshape(1)
    count, length, _ = token_inputs.shape
    states = state_out.shape[3]
    write = state_in.reshape(count, length, states)
    read = state_out.reshape(count, length, states)
    state = prefix_state.reshape(-1, states)

    decay = jnp.swapaxes(log_decay, 1, 2)
    tails = [prefix_tail] + [shift(prefix_tail, by) for by in range(1, SPAN)]
    packed = pack(prefix_keys, prefix_values)
    packs = [packed] + [shift(packed, by) for by in range(1, SPAN)]
    carried = carry(after(resp_length, packed, *tails), decay, out_cotangent, read)
    carry_two = shift(carried, -2)
    carry_last = lax.ppermute(carried, "dp", [(i, (i - (1 if i % 2 else 3)) % devices) for i in range(devices)])
    g_inputs, g_tail, conv, g_read = mamba(
        rank, resp_prefix, after(resp_length, carried), skip_gain, token_inputs, tails, conv_weight, write, read, decay, out_cotangent, devices
    )
    steps = [by for by in (4, 8, 1, 2) if by < devices]
    while 2 * max(steps) < devices:
        steps.append(2 * max(steps))
    whole = devices & (devices - 1) == 0
    swaps = iter(steps if whole else [])

    def next_step():
        by = next(swaps, None)
        return jnp.zeros_like(conv) if by is None else swap(conv, by)

    moved = next_step()
    g_queries, *backs = attention(
        rank, resp_prefix, resp_length, prefix_length, queries, attn_cotangent, own_keys, own_values, packs, g_tail, devices
    )
    *backs, moved, carry_two = lax.optimization_barrier((*backs, moved, carry_two))
    conv = conv + moved
    moved = next_step()
    carry_relay = swap(carry_two, 1)
    backs = [backs[0]] + [shift(backs[by], -by) for by in range(1, SPAN)]
    g_state, *reads = owner(rank, resp_prefix, state, [carried, carry_two, carry_relay, carry_last], devices)
    *reads, moved = lax.optimization_barrier((*reads, moved))
    conv = conv + moved
    moved = next_step()
    reads = [reads[0]] + [shift(reads[by], by) for by in range(1, SPAN)]
    sums = sum_back(backs, prefix_tail.shape)
    *sums, moved, r0, r1, r2, r3 = lax.optimization_barrier((*sums, moved, *reads))
    g_prefix_keys, g_prefix_values, g_prefix_tail = sums
    conv = conv + moved
    for by in swaps:
        conv = conv + swap(conv, by)
    if not whole:
        conv = lax.psum(conv, "dp")
    for part in (r0, r1, r2, r3):
        g_read = g_read + part.astype(F32)
    token_total = count * length * devices
    grad_conv = conv * (1.0 / math.sqrt(token_total))
    return (
        g_inputs,
        g_read.astype(BF16).reshape(state_out.shape),
        g_queries,
        g_state.reshape(prefix_state.shape),
        jnp.swapaxes(g_prefix_tail, 0, 1),
        g_prefix_keys,
        g_prefix_values,
        grad_conv,
    )


def solution(mesh):
    split = ("groups", "dp")
    placed = (
        P(split, None, None),
        P(split, None, None, None),
        P(split, None, None, None),
        P(split, None, None),
        P(),
        P(),
        P(split, None, None),
        P(split, None, None),
        P(split, None, None),
        P(split, None, None),
        P(split, None, None),
        P(split),
        P("groups"),
        P(split, None, None, None),
        P(split, None, None),
        P(split, None, None),
        P(split, None, None),
        P("groups"),
    )
    return jax.shard_map(
        on_device,
        mesh=mesh,
        in_specs=placed,
        out_specs=(
            P(split, None, None),
            P(split, None, None, None),
            P(split, None, None),
            P(split, None, None, None),
            P(split, None, None),
            P(split, None, None),
            P(split, None, None),
            P("groups", None),
        ),
        check_vma=False,
    )
```

```python
import functools
import math

import jax
import jax.numpy as jnp
from jax import lax
from jax.experimental import pallas as pl
from jax.experimental.pallas import tpu as pltpu
from jax.sharding import PartitionSpec as P

ATT_HEADS = 32
KV_HEADS = 4
ATT_DIM = 128
HEADS = 32
HEAD_DIM = 64
SPAN = 4
REPEAT = ATT_HEADS // KV_HEADS
NEG_FILL = -1e30
F32 = jnp.float32
BF16 = jnp.bfloat16

SMEM = pl.BlockSpec(memory_space=pltpu.SMEM)
VMEM = pl.BlockSpec(memory_space=pltpu.VMEM)


def shift(value, by):
    length = lax.axis_size("dp")
    return lax.ppermute(value, "dp", [(i, (i + by) % length) for i in range(length)])


def nt(a, b):
    return lax.dot_general(a, b, (((1,), (1,)), ((), ())), preferred_element_type=F32)


def tn(a, b):
    return lax.dot_general(a, b, (((0,), (0,)), ((), ())), preferred_element_type=F32)


def nn(a, b):
    return lax.dot_general(a, b, (((1,), (0,)), ((), ())), preferred_element_type=F32)


def pack_kernel(keys, values, tail, out, rows8):
    rows = keys.shape[1]
    out[0, 0:rows, :] = keys[0]
    out[1, 0:rows, :] = values[0]
    rows8[...] = jnp.zeros_like(rows8)
    rows8[5:8, :] = tail[0].astype(F32)
    for half in range(2):
        upper = rows8[:, half * 1024 : half * 1024 + 512]
        lower = rows8[:, half * 1024 + 512 : half * 1024 + 1024]
        out[half, rows : rows + 16, :] = jnp.concatenate([upper, lower], axis=0).astype(BF16)


def pack(prefix_keys, prefix_values, prefix_tail):
    rows, width = prefix_keys.shape[1:]
    return pl.pallas_call(
        pack_kernel,
        out_shape=jax.ShapeDtypeStruct((2, rows + 16, width), BF16),
        in_specs=[VMEM] * 3,
        out_specs=VMEM,
        scratch_shapes=[pltpu.VMEM((8, prefix_tail.shape[2]), F32)],
        name="pack_prefix",
    )(prefix_keys, prefix_values, prefix_tail)


def running_sum(log_decay):
    heads, length = log_decay.shape
    row = lax.broadcasted_iota(jnp.int32, (length, length), 0)
    col = lax.broadcasted_iota(jnp.int32, (length, length), 1)
    upper = (row <= col).astype(F32)
    rows = lax.dot_general(
        log_decay,
        upper,
        (((1,), (0,)), ((), ())),
        precision=lax.Precision.HIGHEST,
        preferred_element_type=F32,
    )
    return jnp.concatenate([rows, jnp.zeros((128 - heads, length), F32)], axis=0).T, rows


def carry_kernel(resp_length, log_decay, cotangent, read, out):
    length = cotangent.shape[1]
    width = cotangent.shape[2]
    live_to = resp_length[pl.program_id(0)]
    raised = jnp.exp(running_sum(log_decay[0])[0])
    live = lax.broadcasted_iota(jnp.int32, (length, 2 * HEAD_DIM), 0) < live_to
    first = lax.broadcasted_iota(jnp.int32, (length, 2 * HEAD_DIM), 1) < HEAD_DIM
    for pair in range(width // (2 * HEAD_DIM)):
        lanes = slice(pair * 2 * HEAD_DIM, (pair + 1) * 2 * HEAD_DIM)
        factor = jnp.where(first, raised[:, 2 * pair : 2 * pair + 1], raised[:, 2 * pair + 1 : 2 * pair + 2])
        factor = jnp.where(live, factor, 0.0)
        out[0, :, lanes] = (factor * cotangent[0, :, lanes].astype(F32)).astype(BF16)
    out[0, :, width:] = read[0]


def carry(resp_length, log_decay, out_cotangent, state_out):
    count, length, width = out_cotangent.shape
    heads = log_decay.shape[1]
    states = state_out.shape[2]
    return pl.pallas_call(
        carry_kernel,
        grid=(count,),
        out_shape=jax.ShapeDtypeStruct((count, length, width + states), BF16),
        in_specs=[
            SMEM,
            pl.BlockSpec((1, heads, length), lambda r: (r, 0, 0)),
            pl.BlockSpec((1, length, width), lambda r: (r, 0, 0)),
            pl.BlockSpec((1, length, states), lambda r: (r, 0, 0)),
        ],
        out_specs=pl.BlockSpec((1, length, width + states), lambda r: (r, 0, 0)),
        name="carry_cotangent",
    )(resp_length, log_decay, out_cotangent, state_out)


def relayed(rank):
    even = rank % 2 == 0
    return 0, 2, jnp.where(even, 1, 3), jnp.where(even, 3, 1)


def swap(value, by):
    return lax.ppermute(value, "dp", [(i, i ^ by) for i in range(lax.axis_size("dp"))])


def two_and_last(value, sign):
    length = lax.axis_size("dp")
    if sign > 0:
        pairs = [(i, (i + (3 if i % 2 else 1)) % length) for i in range(length)]
    else:
        pairs = [(i, (i - (1 if i % 2 else 3)) % length) for i in range(length)]
    return shift(value, 2 * sign), lax.ppermute(value, "dp", pairs)


def after(value, *others):
    return lax.optimization_barrier((value,) + others)[0]


def distance_to(rank, owner, devices):
    gap = rank - owner
    return jnp.where(gap < 0, gap + devices, gap)


def mamba_kernel(
    devices,
    rank_ref,
    resp_prefix,
    resp_length,
    skip_gain,
    inputs,
    pack0,
    pack1,
    pack2,
    pack3,
    conv_weight,
    write,
    read,
    log_decay,
    cotangent,
    g_inputs,
    g_tail,
    g_conv,
    g_read,
    padded,
    shifted,
    inner,
):
    resp = pl.program_id(0)
    length = inputs.shape[1]
    width = inputs.shape[2]
    taps = conv_weight.shape[0]
    rank = rank_ref[0]
    live_to = resp_length[resp]
    gap = distance_to(rank, resp_prefix[2 * rank + resp], devices)
    for step, packed in zip(relayed(rank), (pack0, pack1, pack2, pack3)):

        @pl.when(gap == step)
        def _(packed=packed):
            for half in range(2):
                rows = packed[half].astype(F32)
                for part in range(2):
                    lo = half * 1024 + part * 512
                    padded[0:8, lo : lo + 512] = rows[8 * part : 8 * part + 8]

    padded[8 : 8 + length, :] = inputs[0].astype(F32)
    decay_sum, decay_rows = running_sum(log_decay[0])
    s_index = lax.broadcasted_iota(jnp.int32, (length, length), 0)
    t_index = lax.broadcasted_iota(jnp.int32, (length, length), 1)
    causal = s_index <= t_index
    mixing = nt(write[0], read[0])
    live = lax.broadcasted_iota(jnp.int32, (length, 2 * HEAD_DIM), 0) < live_to
    first = lax.broadcasted_iota(jnp.int32, (length, 2 * HEAD_DIM), 1) < HEAD_DIM
    inner[...] = jnp.zeros_like(inner)
    for pair in range(width // (2 * HEAD_DIM)):
        lo = pair * 2 * HEAD_DIM
        lanes = slice(lo, lo + 2 * HEAD_DIM)
        weight = [conv_weight[k : k + 1, lanes] for k in range(taps)]
        mixed = weight[0] * padded[5 : 5 + length, lanes]
        for k in range(1, taps):
            mixed = mixed + weight[k] * padded[5 + k : 5 + k + length, lanes]
        gate = jax.nn.sigmoid(mixed)
        activated = (mixed * gate).astype(BF16)
        d_out = jnp.where(live, cotangent[0, :, lanes].astype(F32), 0.0)
        both = jnp.concatenate(
            [jnp.where(first, d_out, 0.0).astype(BF16), jnp.where(first, 0.0, d_out).astype(BF16)], axis=0
        )
        d_weights = nt(activated, both)
        decays = []
        for head in (2 * pair, 2 * pair + 1):
            lag = decay_rows[head : head + 1, :] - decay_sum[:, head : head + 1]
            decays.append(jnp.exp(jnp.where(causal, lag, NEG_FILL)))
        weights = jnp.concatenate([(d * mixing).astype(BF16) for d in decays], axis=1)
        inner[...] += decays[0] * d_weights[:, :length] + decays[1] * d_weights[:, length:]
        gain = jnp.where(first[0:1], skip_gain[2 * pair], skip_gain[2 * pair + 1])
        d_act = nn(weights, both) + gain * d_out
        d_mixed = d_act * (gate * (1.0 + mixed * (1.0 - gate)))
        shifted[0:8, lanes] = jnp.zeros((8, 2 * HEAD_DIM), F32)
        shifted[8 : 8 + length, lanes] = d_mixed
        shifted[8 + length : 16 + length, lanes] = jnp.zeros((8, 2 * HEAD_DIM), F32)
        total = weight[0] * shifted[11 : 11 + length, lanes]
        early = weight[0] * shifted[8:16, lanes]
        for k in range(1, taps):
            total = total + weight[k] * shifted[11 - k : 11 - k + length, lanes]
            early = early + weight[k] * shifted[8 - k : 16 - k, lanes]
        g_inputs[0, :, lanes] = total.astype(BF16)
        g_tail[0, lo // 512, :, lo % 512 : lo % 512 + 2 * HEAD_DIM] = early
        rows = [
            jnp.sum(d_mixed * padded[5 + k : 5 + k + length, lanes], axis=0, keepdims=True) for k in range(taps)
        ]
        rows = jnp.concatenate(rows, axis=0)


        @pl.when(resp == 0)
        def _(rows=rows, lanes=lanes):
            g_conv[:, lanes] = rows

        @pl.when(resp > 0)
        def _(rows=rows, lanes=lanes):
            g_conv[:, lanes] += rows

    g_read[0] = tn(inner[...].astype(BF16), write[0])


def mamba(rank, resp_prefix, resp_length, skip_gain, inputs, packs, conv_weight, write, read, log_decay, cotangent, devices):
    count, length, width = inputs.shape
    heads = log_decay.shape[1]
    states = read.shape[2]
    taps = conv_weight.shape[0]
    whole = pl.BlockSpec((2, 16, packs[0].shape[2]), lambda r: (0, (packs[0].shape[1] - 16) // 16, 0))
    return pl.pallas_call(
        functools.partial(mamba_kernel, devices),
        grid=(count,),
        out_shape=[
            jax.ShapeDtypeStruct((count, length, width), BF16),
            jax.ShapeDtypeStruct((count, 4, 8, 512), F32),
            jax.ShapeDtypeStruct((taps, width), F32),
            jax.ShapeDtypeStruct((count, length, states), F32),
        ],
        in_specs=[
            SMEM,
            SMEM,
            SMEM,
            SMEM,
            pl.BlockSpec((1, length, width), lambda r: (r, 0, 0)),
            whole,
            whole,
            whole,
            whole,
            pl.BlockSpec((taps, width), lambda r: (0, 0)),
            pl.BlockSpec((1, length, states), lambda r: (r, 0, 0)),
            pl.BlockSpec((1, length, states), lambda r: (r, 0, 0)),
            pl.BlockSpec((1, heads, length), lambda r: (r, 0, 0)),
            pl.BlockSpec((1, length, width), lambda r: (r, 0, 0)),
        ],
        out_specs=[
            pl.BlockSpec((1, length, width), lambda r: (r, 0, 0)),
            pl.BlockSpec((1, 4, 8, 512), lambda r: (r, 0, 0, 0)),
            pl.BlockSpec((taps, width), lambda r: (0, 0)),
            pl.BlockSpec((1, length, states), lambda r: (r, 0, 0)),
        ],
        scratch_shapes=[
            pltpu.VMEM((length + 8, width), F32),
            pltpu.VMEM((length + 16, width), F32),
            pltpu.VMEM((length, length), F32),
        ],
        compiler_params=pltpu.CompilerParams(vmem_limit_bytes=58 * 2**20),
        cost_estimate=pl.CostEstimate(flops=2 * 10**9, bytes_accessed=8 * 2**20, transcendentals=10**6),
        name="mamba_grads",
    )(rank, resp_prefix, resp_length, skip_gain, inputs, *packs, conv_weight, write, read, log_decay, cotangent)


def attention_kernel(
    devices,
    rank_ref,
    resp_prefix,
    resp_length,
    prefix_length,
    queries,
    cotangent,
    own_keys,
    own_values,
    pack0,
    pack1,
    pack2,
    pack3,
    g_tail,
    g_queries,
    back0,
    back1,
    back2,
    back3,
    keys,
    values,
    kept,
):
    resp = pl.program_id(1)
    length = queries.shape[1]
    rows = keys.shape[0] - length
    rank = rank_ref[0]
    prefix = resp_prefix[2 * rank + resp]
    pref_len = prefix_length[prefix]
    live_to = resp_length[resp]
    scale = 1.0 / math.sqrt(ATT_DIM)
    gap = distance_to(rank, prefix, devices)
    for step, packed in zip(relayed(rank), (pack0, pack1, pack2, pack3)):

        @pl.when(gap == step)
        def _(packed=packed):
            keys[0:rows, :] = packed[0, 0:rows, :]
            values[0:rows, :] = packed[1, 0:rows, :]

    keys[rows : rows + length, :] = own_keys[0]
    values[rows : rows + length, :] = own_values[0]
    j_index = lax.broadcasted_iota(jnp.int32, (rows + length, 2 * length), 0)
    t_index = lax.broadcasted_iota(jnp.int32, (rows + length, 2 * length), 1)
    t_index = jnp.where(t_index >= length, t_index - length, t_index)
    bound = jnp.where(j_index < rows, pref_len, t_index + rows + 1)
    bias = jnp.where(j_index < bound, 0.0, NEG_FILL)
    live = lax.broadcasted_iota(jnp.int32, (length, ATT_DIM), 0) < live_to
    all_keys = keys[...]
    all_values = values[...]
    g_keys = jnp.zeros((rows, ATT_DIM), F32)
    g_values = jnp.zeros((rows, ATT_DIM), F32)
    for duo in range(REPEAT // 2):
        spans = [slice((2 * duo + i) * ATT_DIM, (2 * duo + i + 1) * ATT_DIM) for i in range(2)]
        query = jnp.concatenate([queries[0, :, span] for span in spans], axis=0)
        d_out = jnp.concatenate(
            [jnp.where(live, cotangent[0, :, span].astype(F32), 0.0).astype(BF16) for span in spans], axis=0
        )
        scores = nt(all_keys, query) * (scale * math.log2(math.e)) + bias
        top = jnp.max(scores, axis=0, keepdims=True)
        raised = jnp.exp2(scores - top)
        probs = raised * (1.0 / jnp.sum(raised, axis=0, keepdims=True))
        probs_low = probs.astype(BF16)
        d_probs = nt(all_values, d_out)
        delta = jnp.sum(probs * d_probs, axis=0, keepdims=True)
        d_scores = (probs * (d_probs - delta)).astype(BF16)
        g_query = tn(d_scores, all_keys) * scale
        for i, span in enumerate(spans):
            g_queries[0, :, span] = g_query[i * length : (i + 1) * length].astype(BF16)
        g_keys = g_keys + nn(d_scores[0:rows], query)
        g_values = g_values + nn(probs_low[0:rows], d_out)

    g_keys = g_keys * scale

    @pl.when(resp == 0)
    def _():
        kept[0] = g_keys
        kept[1] = g_values

    @pl.when(resp == 1)
    def _():
        before = distance_to(rank, resp_prefix[2 * rank], devices)
        for step, back in enumerate((back0, back1, back2, back3)):
            one = jnp.where(before == step, 1.0, 0.0)
            two = jnp.where(gap == step, 1.0, 0.0)
            back[0, 0:rows, :] = (kept[0] * one + g_keys * two).astype(back.dtype)
            back[1, 0:rows, :] = (kept[1] * one + g_values * two).astype(back.dtype)
            for half in range(2):
                tiles = [g_tail[0, part] * one + g_tail[1, part] * two for part in (2 * half, 2 * half + 1)]
                back[half, rows : rows + 16, :] = jnp.concatenate(tiles, axis=0).astype(back.dtype)


def attention(rank, resp_prefix, resp_length, prefix_length, queries, cotangent, own_keys, own_values, packs, g_tail, devices):
    count, length, width = queries.shape
    rows = packs[0].shape[1] - 16
    group = REPEAT * ATT_DIM
    packed = pl.BlockSpec((2, rows, ATT_DIM), lambda h, r: (0, 0, h))
    back_block = pl.BlockSpec((2, rows + 16, ATT_DIM), lambda h, r: (0, 0, h))
    back = (2, rows + 16, KV_HEADS * ATT_DIM)
    return pl.pallas_call(
        functools.partial(attention_kernel, devices),
        grid=(KV_HEADS, count),
        out_shape=[
            jax.ShapeDtypeStruct((count, length, width), BF16),
            jax.ShapeDtypeStruct(back, F32),
            jax.ShapeDtypeStruct(back, BF16),
            jax.ShapeDtypeStruct(back, BF16),
            jax.ShapeDtypeStruct(back, BF16),
        ],
        in_specs=[
            SMEM,
            SMEM,
            SMEM,
            SMEM,
            pl.BlockSpec((1, length, group), lambda h, r: (r, 0, h)),
            pl.BlockSpec((1, length, group), lambda h, r: (r, 0, h)),
            pl.BlockSpec((1, length, ATT_DIM), lambda h, r: (r, 0, h)),
            pl.BlockSpec((1, length, ATT_DIM), lambda h, r: (r, 0, h)),
            packed,
            packed,
            packed,
            packed,
            pl.BlockSpec((count, 4, 8, ATT_DIM), lambda h, r: (0, 0, 0, h)),
        ],
        out_specs=[
            pl.BlockSpec((1, length, group), lambda h, r: (r, 0, h)),
            back_block,
            back_block,
            back_block,
            back_block,
        ],
        scratch_shapes=[
            pltpu.VMEM((rows + length, ATT_DIM), BF16),
            pltpu.VMEM((rows + length, ATT_DIM), BF16),
            pltpu.VMEM((2, rows, ATT_DIM), F32),
        ],
        compiler_params=pltpu.CompilerParams(vmem_limit_bytes=58 * 2**20),
        cost_estimate=pl.CostEstimate(flops=4 * 10**9, bytes_accessed=8 * 2**20, transcendentals=2 * 10**6),
        name="attention_grads",
    )(rank, resp_prefix, resp_length, prefix_length, queries, cotangent, own_keys, own_values, *packs, g_tail)


def owner_kernel(devices, rank_ref, resp_prefix, state, car0, car1, car2, car3, g_state, dr0, dr1, dr2, dr3, total, parts):
    rank = rank_ref[0]
    even = rank % 2 == 0
    width = state.shape[0]
    chunk = 512
    total[...] = jnp.zeros_like(total)
    for slot, (step, carried) in enumerate(
        zip((0, 2, jnp.where(even, 3, 1), jnp.where(even, 1, 3)), (car0, car1, car2, car3))
    ):
        sender = rank + step
        sender = jnp.where(sender >= devices, sender - devices, sender)
        for resp in range(2):
            mine = resp_prefix[2 * sender + resp] == rank

            @pl.when(mine)
            def _(carried=carried, slot=slot, resp=resp):
                read = carried[resp, :, width:]
                acc = None
                for at in range(0, width, chunk):
                    piece = carried[resp, :, at : at + chunk]
                    term = nn(piece, state[at : at + chunk, :])
                    acc = term if acc is None else acc + term
                    total[at : at + chunk, :] += tn(piece, read)
                parts[slot, resp] = acc

            @pl.when(jnp.logical_not(mine))
            def _(slot=slot, resp=resp):
                parts[slot, resp] = jnp.zeros(parts.shape[2:], F32)

    g_state[...] = total[...].astype(BF16)
    dr0[...] = parts[0]
    dr2[...] = parts[1].astype(BF16)

    @pl.when(even)
    def _():
        dr3[...] = parts[2].astype(BF16)
        dr1[...] = parts[3].astype(BF16)

    @pl.when(jnp.logical_not(even))
    def _():
        dr1[...] = parts[2].astype(BF16)
        dr3[...] = parts[3].astype(BF16)


def owner(rank, resp_prefix, state, carried, devices):
    width, states = state.shape
    count, length = carried[0].shape[:2]
    return pl.pallas_call(
        functools.partial(owner_kernel, devices),
        out_shape=[jax.ShapeDtypeStruct((width, states), BF16), jax.ShapeDtypeStruct((count, length, states), F32)]
        + [jax.ShapeDtypeStruct((count, length, states), BF16)] * 3,
        in_specs=[SMEM, SMEM] + [VMEM] * 5,
        out_specs=[VMEM] * 5,
        scratch_shapes=[pltpu.VMEM((width, states), F32), pltpu.VMEM((SPAN, count, length, states), F32)],
        compiler_params=pltpu.CompilerParams(vmem_limit_bytes=24 * 2**20),
        cost_estimate=pl.CostEstimate(flops=2 * 10**9, bytes_accessed=8 * 2**20, transcendentals=0),
        name="owner_state",
    )(rank, resp_prefix, state, *carried)


def sum_kernel(back0, back1, back2, back3, g_keys, g_values, g_tail):
    rows = g_keys.shape[1]
    for half, out in enumerate((g_keys, g_values)):
        total = back0[half]
        for back in (back1, back2, back3):
            total = total + back[half].astype(F32)
        out[0] = total[0:rows]
        for part in range(2):
            lo = half * 1024 + part * 512
            g_tail[:, 0, lo : lo + 512] = total[rows + 8 * part : rows + 8 * part + 3]


def sum_back(backs, tail_shape):
    rows = backs[0].shape[1] - 16
    width = backs[0].shape[2]
    return pl.pallas_call(
        sum_kernel,
        out_shape=[
            jax.ShapeDtypeStruct((1, rows, width), F32),
            jax.ShapeDtypeStruct((1, rows, width), F32),
            jax.ShapeDtypeStruct((tail_shape[1], 1, tail_shape[2]), F32),
        ],
        in_specs=[VMEM] * 4,
        out_specs=[VMEM] * 3,
        name="sum_prefix",
    )(*backs)


def on_device(
    token_inputs,
    state_in,
    state_out,
    log_decay,
    skip_gain,
    conv_weight,
    out_cotangent,
    queries,
    own_keys,
    own_values,
    attn_cotangent,
    resp_length,
    resp_prefix,
    prefix_state,
    prefix_tail,
    prefix_keys,
    prefix_values,
    prefix_length,
):
    devices = lax.axis_size("dp")
    rank = lax.axis_index("dp").astype(jnp.int32).reshape(1)
    count, length, _ = token_inputs.shape
    states = state_out.shape[3]
    write = state_in.reshape(count, length, states)
    read = state_out.reshape(count, length, states)
    state = prefix_state.reshape(-1, states)

    decay = jnp.swapaxes(log_decay, 1, 2)
    packed = pack(prefix_keys, prefix_values, prefix_tail)
    pack_two, pack_last = two_and_last(packed, 1)
    carried = carry(after(resp_length, packed), decay, out_cotangent, read)
    pack_two, pack_last, carried = lax.optimization_barrier((pack_two, pack_last, carried))
    carry_two, carry_last = two_and_last(carried, -1)
    packs = [packed, pack_two, swap(pack_two, 1), pack_last]
    g_inputs, g_tail, conv, g_read = mamba(
        rank, resp_prefix, resp_length, skip_gain, token_inputs, packs, conv_weight, write, read, decay, out_cotangent, devices
    )
    steps = [by for by in (2, 1, 4, 8) if by < devices]
    while 2 * max(steps) < devices:
        steps.append(2 * max(steps))
    whole = devices & (devices - 1) == 0
    swaps = iter(steps if whole else [])

    def next_step():
        by = next(swaps, None)
        return jnp.zeros_like(conv) if by is None else swap(conv, by)

    moved = next_step()
    g_queries, *backs = attention(
        rank, resp_prefix, resp_length, prefix_length, queries, attn_cotangent, own_keys, own_values, packs, g_tail, devices
    )
    *backs, moved, carry_two = lax.optimization_barrier((*backs, moved, carry_two))
    conv = conv + moved
    moved = next_step()
    carry_relay = swap(carry_two, 1)
    backs = [backs[0]] + [shift(backs[by], -by) for by in range(1, SPAN)]
    g_state, *reads = owner(rank, after(resp_prefix, moved), state, [carried, carry_two, carry_relay, carry_last], devices)
    conv = conv + moved
    moved = next_step()
    reads = [reads[0]] + [shift(reads[by], by) for by in range(1, SPAN)]
    sums = sum_back(backs, prefix_tail.shape)
    *sums, moved, r0, r1, r2, r3 = lax.optimization_barrier((*sums, moved, *reads))
    g_prefix_keys, g_prefix_values, g_prefix_tail = sums
    conv = conv + moved
    for by in swaps:
        conv = conv + swap(conv, by)
    if not whole:
        conv = lax.psum(conv, "dp")
    for part in (r0, r1, r2, r3):
        g_read = g_read + part.astype(F32)
    token_total = count * length * devices
    grad_conv = conv * (1.0 / math.sqrt(token_total))
    return (
        g_inputs,
        g_read.astype(BF16).reshape(state_out.shape),
        g_queries,
        g_state.reshape(prefix_state.shape),
        jnp.swapaxes(g_prefix_tail, 0, 1),
        g_prefix_keys,
        g_prefix_values,
        grad_conv,
    )


def solution(mesh):
    split = ("groups", "dp")
    placed = (
        P(split, None, None),
        P(split, None, None, None),
        P(split, None, None, None),
        P(split, None, None),
        P(),
        P(),
        P(split, None, None),
        P(split, None, None),
        P(split, None, None),
        P(split, None, None),
        P(split, None, None),
        P(split),
        P("groups"),
        P(split, None, None, None),
        P(split, None, None),
        P(split, None, None),
        P(split, None, None),
        P("groups"),
    )
    return jax.shard_map(
        on_device,
        mesh=mesh,
        in_specs=placed,
        out_specs=(
            P(split, None, None),
            P(split, None, None, None),
            P(split, None, None),
            P(split, None, None, None),
            P(split, None, None),
            P(split, None, None),
            P(split, None, None),
            P("groups", None),
        ),
        check_vma=False,
    )
```

```python
import functools
import math

import jax
import jax.numpy as jnp
from jax import lax
from jax.experimental import pallas as pl
from jax.experimental.pallas import tpu as pltpu
from jax.sharding import PartitionSpec as P

ATT_HEADS = 32
KV_HEADS = 4
ATT_DIM = 128
HEADS = 32
HEAD_DIM = 64
SPAN = 4
REPEAT = ATT_HEADS // KV_HEADS
TOGETHER = 2
NEG_FILL = -1e30
F32 = jnp.float32
BF16 = jnp.bfloat16

SMEM = pl.BlockSpec(memory_space=pltpu.SMEM)
VMEM = pl.BlockSpec(memory_space=pltpu.VMEM)


def shift(value, by):
    length = lax.axis_size("dp")
    return lax.ppermute(value, "dp", [(i, (i + by) % length) for i in range(length)])


def nt(a, b):
    return lax.dot_general(a, b, (((1,), (1,)), ((), ())), preferred_element_type=F32)


def tn(a, b):
    return lax.dot_general(a, b, (((0,), (0,)), ((), ())), preferred_element_type=F32)


def nn(a, b):
    return lax.dot_general(a, b, (((1,), (0,)), ((), ())), preferred_element_type=F32)


def pack_kernel(keys, values, tail, out, rows8):
    rows = keys.shape[1]
    out[0, 0:rows, :] = keys[0]
    out[1, 0:rows, :] = values[0]
    rows8[...] = jnp.zeros_like(rows8)
    rows8[5:8, :] = tail[0].astype(F32)
    for half in range(2):
        upper = rows8[:, half * 1024 : half * 1024 + 512]
        lower = rows8[:, half * 1024 + 512 : half * 1024 + 1024]
        out[half, rows : rows + 16, :] = jnp.concatenate([upper, lower], axis=0).astype(BF16)


def pack(prefix_keys, prefix_values, prefix_tail):
    rows, width = prefix_keys.shape[1:]
    return pl.pallas_call(
        pack_kernel,
        out_shape=jax.ShapeDtypeStruct((2, rows + 16, width), BF16),
        in_specs=[VMEM] * 3,
        out_specs=VMEM,
        scratch_shapes=[pltpu.VMEM((8, prefix_tail.shape[2]), F32)],
        name="pack_prefix",
    )(prefix_keys, prefix_values, prefix_tail)


def running_sum(log_decay):
    heads, length = log_decay.shape
    row = lax.broadcasted_iota(jnp.int32, (length, length), 0)
    col = lax.broadcasted_iota(jnp.int32, (length, length), 1)
    upper = (row <= col).astype(F32)
    rows = lax.dot_general(
        log_decay,
        upper,
        (((1,), (0,)), ((), ())),
        precision=lax.Precision.HIGHEST,
        preferred_element_type=F32,
    )
    return jnp.concatenate([rows, jnp.zeros((128 - heads, length), F32)], axis=0).T, rows


def carry_kernel(resp_length, log_decay, cotangent, read, out):
    length = cotangent.shape[1]
    width = cotangent.shape[2]
    live_to = resp_length[pl.program_id(0)]
    raised = jnp.exp(running_sum(log_decay[0])[0])
    live = lax.broadcasted_iota(jnp.int32, (length, 2 * HEAD_DIM), 0) < live_to
    first = lax.broadcasted_iota(jnp.int32, (length, 2 * HEAD_DIM), 1) < HEAD_DIM
    for pair in range(width // (2 * HEAD_DIM)):
        lanes = slice(pair * 2 * HEAD_DIM, (pair + 1) * 2 * HEAD_DIM)
        factor = jnp.where(first, raised[:, 2 * pair : 2 * pair + 1], raised[:, 2 * pair + 1 : 2 * pair + 2])
        factor = jnp.where(live, factor, 0.0)
        out[0, :, lanes] = (factor * cotangent[0, :, lanes].astype(F32)).astype(BF16)
    out[0, :, width:] = read[0]


def carry(resp_length, log_decay, out_cotangent, state_out):
    count, length, width = out_cotangent.shape
    heads = log_decay.shape[1]
    states = state_out.shape[2]
    return pl.pallas_call(
        carry_kernel,
        grid=(count,),
        out_shape=jax.ShapeDtypeStruct((count, length, width + states), BF16),
        in_specs=[
            SMEM,
            pl.BlockSpec((1, heads, length), lambda r: (r, 0, 0)),
            pl.BlockSpec((1, length, width), lambda r: (r, 0, 0)),
            pl.BlockSpec((1, length, states), lambda r: (r, 0, 0)),
        ],
        out_specs=pl.BlockSpec((1, length, width + states), lambda r: (r, 0, 0)),
        name="carry_cotangent",
    )(resp_length, log_decay, out_cotangent, state_out)


def relayed(rank):
    even = rank % 2 == 0
    return 0, 2, jnp.where(even, 1, 3), jnp.where(even, 3, 1)


def swap(value, by):
    return lax.ppermute(value, "dp", [(i, i ^ by) for i in range(lax.axis_size("dp"))])


def behind(length):
    return [(i, (i - (1 if i % 2 else 3)) % length) for i in range(length)]


def two_and_last(value, sign):
    length = lax.axis_size("dp")
    pairs = behind(length)
    if sign > 0:
        pairs = [(to, origin) for origin, to in pairs]
    return shift(value, 2 * sign), lax.ppermute(value, "dp", pairs)


def after(value, *others):
    return lax.optimization_barrier((value,) + others)[0]


def distance_to(rank, owner, devices):
    gap = rank - owner
    return jnp.where(gap < 0, gap + devices, gap)


def mamba_kernel(
    devices,
    rank_ref,
    resp_prefix,
    resp_length,
    skip_gain,
    inputs,
    pack0,
    pack1,
    pack2,
    pack3,
    conv_weight,
    write,
    read,
    log_decay,
    cotangent,
    g_inputs,
    g_tail,
    g_conv,
    g_read,
    padded,
    shifted,
):
    resp = pl.program_id(0)
    length = inputs.shape[1]
    width = inputs.shape[2]
    taps = conv_weight.shape[0]
    rank = rank_ref[0]
    live_to = resp_length[resp]
    gap = distance_to(rank, resp_prefix[2 * rank + resp], devices)
    for step, packed in zip(relayed(rank), (pack0, pack1, pack2, pack3)):

        @pl.when(gap == step)
        def _(packed=packed):
            for half in range(2):
                rows = packed[half].astype(F32)
                for part in range(2):
                    lo = half * 1024 + part * 512
                    padded[0:8, lo : lo + 512] = rows[8 * part : 8 * part + 8]

    padded[8 : 8 + length, :] = inputs[0].astype(F32)
    decay_sum, decay_rows = running_sum(log_decay[0])
    s_index = lax.broadcasted_iota(jnp.int32, (length, length), 0)
    t_index = lax.broadcasted_iota(jnp.int32, (length, length), 1)
    causal = s_index <= t_index
    mixing = nt(write[0], read[0])
    live = lax.broadcasted_iota(jnp.int32, (length, 2 * HEAD_DIM), 0) < live_to
    first = lax.broadcasted_iota(jnp.int32, (length, 2 * HEAD_DIM), 1) < HEAD_DIM
    inner = jnp.zeros((length, length), F32)
    for pair in range(width // (2 * HEAD_DIM)):
        lo = pair * 2 * HEAD_DIM
        lanes = slice(lo, lo + 2 * HEAD_DIM)
        weight = [conv_weight[k : k + 1, lanes] for k in range(taps)]
        mixed = weight[0] * padded[5 : 5 + length, lanes]
        for k in range(1, taps):
            mixed = mixed + weight[k] * padded[5 + k : 5 + k + length, lanes]
        gate = jax.nn.sigmoid(mixed)
        activated = (mixed * gate).astype(BF16)
        d_out = jnp.where(live, cotangent[0, :, lanes].astype(F32), 0.0)
        both = jnp.concatenate(
            [jnp.where(first, d_out, 0.0).astype(BF16), jnp.where(first, 0.0, d_out).astype(BF16)], axis=0
        )
        d_weights = nt(activated, both)
        decays = []
        for head in (2 * pair, 2 * pair + 1):
            lag = decay_rows[head : head + 1, :] - decay_sum[:, head : head + 1]
            decays.append(jnp.exp(jnp.where(causal, lag, NEG_FILL)))
        weights = jnp.concatenate([(d * mixing).astype(BF16) for d in decays], axis=1)
        inner = inner + decays[0] * d_weights[:, :length] + decays[1] * d_weights[:, length:]
        gain = jnp.where(first[0:1], skip_gain[2 * pair], skip_gain[2 * pair + 1])
        d_act = nn(weights, both) + gain * d_out
        d_mixed = d_act * (gate * (1.0 + mixed * (1.0 - gate)))
        shifted[0:8, lanes] = jnp.zeros((8, 2 * HEAD_DIM), F32)
        shifted[8 : 8 + length, lanes] = d_mixed
        shifted[8 + length : 16 + length, lanes] = jnp.zeros((8, 2 * HEAD_DIM), F32)
        total = weight[0] * shifted[11 : 11 + length, lanes]
        early = weight[0] * shifted[8:16, lanes]
        for k in range(1, taps):
            total = total + weight[k] * shifted[11 - k : 11 - k + length, lanes]
            early = early + weight[k] * shifted[8 - k : 16 - k, lanes]
        g_inputs[0, :, lanes] = total.astype(BF16)
        g_tail[0, lo // 512, :, lo % 512 : lo % 512 + 2 * HEAD_DIM] = early
        rows = [
            jnp.sum(d_mixed * padded[5 + k : 5 + k + length, lanes], axis=0, keepdims=True) for k in range(taps)
        ]
        rows = jnp.concatenate(rows, axis=0)

        g_conv[:, lanes] = rows + jnp.where(resp == 0, 0.0, g_conv[:, lanes])

    g_read[0] = tn(inner.astype(BF16), write[0])


def mamba(rank, resp_prefix, resp_length, skip_gain, inputs, packs, conv_weight, write, read, log_decay, cotangent, devices):
    count, length, width = inputs.shape
    heads = log_decay.shape[1]
    states = read.shape[2]
    taps = conv_weight.shape[0]
    whole = pl.BlockSpec((2, 16, packs[0].shape[2]), lambda r: (0, (packs[0].shape[1] - 16) // 16, 0))
    return pl.pallas_call(
        functools.partial(mamba_kernel, devices),
        grid=(count,),
        out_shape=[
            jax.ShapeDtypeStruct((count, length, width), BF16),
            jax.ShapeDtypeStruct((count, 4, 8, 512), F32),
            jax.ShapeDtypeStruct((taps, width), F32),
            jax.ShapeDtypeStruct((count, length, states), F32),
        ],
        in_specs=[
            SMEM,
            SMEM,
            SMEM,
            SMEM,
            pl.BlockSpec((1, length, width), lambda r: (r, 0, 0)),
            whole,
            whole,
            whole,
            whole,
            pl.BlockSpec((taps, width), lambda r: (0, 0)),
            pl.BlockSpec((1, length, states), lambda r: (r, 0, 0)),
            pl.BlockSpec((1, length, states), lambda r: (r, 0, 0)),
            pl.BlockSpec((1, heads, length), lambda r: (r, 0, 0)),
            pl.BlockSpec((1, length, width), lambda r: (r, 0, 0)),
        ],
        out_specs=[
            pl.BlockSpec((1, length, width), lambda r: (r, 0, 0)),
            pl.BlockSpec((1, 4, 8, 512), lambda r: (r, 0, 0, 0)),
            pl.BlockSpec((taps, width), lambda r: (0, 0)),
            pl.BlockSpec((1, length, states), lambda r: (r, 0, 0)),
        ],
        scratch_shapes=[
            pltpu.VMEM((length + 8, width), F32),
            pltpu.VMEM((length + 16, width), F32),
        ],
        compiler_params=pltpu.CompilerParams(vmem_limit_bytes=58 * 2**20),
        cost_estimate=pl.CostEstimate(flops=2 * 10**9, bytes_accessed=8 * 2**20, transcendentals=10**6),
        name="mamba_grads",
    )(rank, resp_prefix, resp_length, skip_gain, inputs, *packs, conv_weight, write, read, log_decay, cotangent)


def attention_kernel(
    devices,
    rank_ref,
    resp_prefix,
    resp_length,
    prefix_length,
    queries,
    cotangent,
    own_keys,
    own_values,
    pack0,
    pack1,
    pack2,
    pack3,
    g_tail,
    g_queries,
    back0,
    back1,
    back2,
    back3,
    keys,
    values,
    kept,
):
    resp = pl.program_id(1)
    length = queries.shape[1]
    rows = keys.shape[0] - length
    rank = rank_ref[0]
    prefix = resp_prefix[2 * rank + resp]
    pref_len = prefix_length[prefix]
    live_to = resp_length[resp]
    scale = 1.0 / math.sqrt(ATT_DIM)
    gap = distance_to(rank, prefix, devices)
    for step, packed in zip(relayed(rank), (pack0, pack1, pack2, pack3)):

        @pl.when(gap == step)
        def _(packed=packed):
            keys[0:rows, :] = packed[0, 0:rows, :]
            values[0:rows, :] = packed[1, 0:rows, :]

    keys[rows : rows + length, :] = own_keys[0]
    values[rows : rows + length, :] = own_values[0]
    j_index = lax.broadcasted_iota(jnp.int32, (rows + length, length), 0)
    t_index = lax.broadcasted_iota(jnp.int32, (rows + length, length), 1)
    bound = jnp.where(j_index < rows, pref_len, t_index + rows + 1)
    bias = jnp.where(j_index < bound, 0.0, NEG_FILL)
    bias = jnp.concatenate([bias] * TOGETHER, axis=1)
    live = lax.broadcasted_iota(jnp.int32, (length, ATT_DIM), 0) < live_to
    all_keys = keys[...]
    all_values = values[...]
    keys_across = all_keys.T
    g_keys = jnp.zeros((rows, ATT_DIM), F32)
    g_values = jnp.zeros((rows, ATT_DIM), F32)
    for at in range(0, REPEAT, TOGETHER):
        spans = [slice(head * ATT_DIM, (head + 1) * ATT_DIM) for head in range(at, at + TOGETHER)]
        query = jnp.concatenate([queries[0, :, span] for span in spans], axis=0)
        d_out = jnp.concatenate(
            [jnp.where(live, cotangent[0, :, span].astype(F32), 0.0).astype(BF16) for span in spans], axis=0
        )
        scores = nt(all_keys, query) * (scale * math.log2(math.e)) + bias
        top = jnp.max(scores, axis=0, keepdims=True)
        raised = jnp.exp2(scores - top)
        probs = raised * (1.0 / jnp.sum(raised, axis=0, keepdims=True))
        probs_low = probs.astype(BF16)
        d_probs = nt(all_values, d_out)
        delta = jnp.sum(probs * d_probs, axis=0, keepdims=True)
        d_scores = (probs * (d_probs - delta)).astype(BF16)
        g_query = (nn(keys_across, d_scores) * scale).astype(BF16).T
        for i, span in enumerate(spans):
            g_queries[0, :, span] = g_query[i * length : (i + 1) * length]
        g_keys = g_keys + nn(d_scores[0:rows], query)
        g_values = g_values + nn(probs_low[0:rows], d_out)

    g_keys = g_keys * scale

    @pl.when(resp == 0)
    def _():
        kept[0] = g_keys
        kept[1] = g_values

    @pl.when(resp == 1)
    def _():
        before = distance_to(rank, resp_prefix[2 * rank], devices)
        even = rank % 2 == 0
        steps = (0, 2, jnp.where(even, 3, 1), jnp.where(even, 1, 3))
        for step, back in zip(steps, (back0, back1, back2, back3)):
            one = jnp.where(before == step, 1.0, 0.0)
            two = jnp.where(gap == step, 1.0, 0.0)
            back[0, 0:rows, :] = (kept[0] * one + g_keys * two).astype(back.dtype)
            back[1, 0:rows, :] = (kept[1] * one + g_values * two).astype(back.dtype)
            for half in range(2):
                tiles = [g_tail[0, part] * one + g_tail[1, part] * two for part in (2 * half, 2 * half + 1)]
                back[half, rows : rows + 16, :] = jnp.concatenate(tiles, axis=0).astype(back.dtype)


def attention(rank, resp_prefix, resp_length, prefix_length, queries, cotangent, own_keys, own_values, packs, g_tail, devices):
    count, length, width = queries.shape
    rows = packs[0].shape[1] - 16
    group = REPEAT * ATT_DIM
    packed = pl.BlockSpec((2, rows, ATT_DIM), lambda h, r: (0, 0, h))
    back_block = pl.BlockSpec((2, rows + 16, ATT_DIM), lambda h, r: (0, 0, h))
    back = (2, rows + 16, KV_HEADS * ATT_DIM)
    return pl.pallas_call(
        functools.partial(attention_kernel, devices),
        grid=(KV_HEADS, count),
        out_shape=[
            jax.ShapeDtypeStruct((count, length, width), BF16),
            jax.ShapeDtypeStruct(back, F32),
            jax.ShapeDtypeStruct(back, BF16),
            jax.ShapeDtypeStruct(back, BF16),
            jax.ShapeDtypeStruct(back, BF16),
        ],
        in_specs=[
            SMEM,
            SMEM,
            SMEM,
            SMEM,
            pl.BlockSpec((1, length, group), lambda h, r: (r, 0, h)),
            pl.BlockSpec((1, length, group), lambda h, r: (r, 0, h)),
            pl.BlockSpec((1, length, ATT_DIM), lambda h, r: (r, 0, h)),
            pl.BlockSpec((1, length, ATT_DIM), lambda h, r: (r, 0, h)),
            packed,
            packed,
            packed,
            packed,
            pl.BlockSpec((count, 4, 8, ATT_DIM), lambda h, r: (0, 0, 0, h)),
        ],
        out_specs=[
            pl.BlockSpec((1, length, group), lambda h, r: (r, 0, h)),
            back_block,
            back_block,
            back_block,
            back_block,
        ],
        scratch_shapes=[
            pltpu.VMEM((rows + length, ATT_DIM), BF16),
            pltpu.VMEM((rows + length, ATT_DIM), BF16),
            pltpu.VMEM((2, rows, ATT_DIM), F32),
        ],
        compiler_params=pltpu.CompilerParams(vmem_limit_bytes=58 * 2**20),
        cost_estimate=pl.CostEstimate(flops=4 * 10**9, bytes_accessed=8 * 2**20, transcendentals=2 * 10**6),
        name="attention_grads",
    )(rank, resp_prefix, resp_length, prefix_length, queries, cotangent, own_keys, own_values, *packs, g_tail)


def owner_kernel(devices, rank_ref, resp_prefix, state, car0, car1, car2, car3, g_state, dr0, dr1, dr2, dr3, total, parts):
    rank = rank_ref[0]
    even = rank % 2 == 0
    width = state.shape[0]
    chunk = 512
    total[...] = jnp.zeros_like(total)
    for slot, (step, carried) in enumerate(
        zip((0, 2, jnp.where(even, 3, 1), jnp.where(even, 1, 3)), (car0, car1, car2, car3))
    ):
        sender = rank + step
        sender = jnp.where(sender >= devices, sender - devices, sender)
        for resp in range(2):
            mine = resp_prefix[2 * sender + resp] == rank

            @pl.when(mine)
            def _(carried=carried, slot=slot, resp=resp):
                read = carried[resp, :, width:]
                acc = None
                for at in range(0, width, chunk):
                    piece = carried[resp, :, at : at + chunk]
                    term = nn(piece, state[at : at + chunk, :])
                    acc = term if acc is None else acc + term
                    total[at : at + chunk, :] += tn(piece, read)
                parts[slot, resp] = acc

            @pl.when(jnp.logical_not(mine))
            def _(slot=slot, resp=resp):
                parts[slot, resp] = jnp.zeros(parts.shape[2:], F32)

    g_state[...] = total[...].astype(BF16)
    dr0[...] = parts[0]
    dr2[...] = parts[1].astype(BF16)

    @pl.when(even)
    def _():
        dr3[...] = parts[2].astype(BF16)
        dr1[...] = parts[3].astype(BF16)

    @pl.when(jnp.logical_not(even))
    def _():
        dr1[...] = parts[2].astype(BF16)
        dr3[...] = parts[3].astype(BF16)


def owner(rank, resp_prefix, state, carried, devices):
    width, states = state.shape
    count, length = carried[0].shape[:2]
    return pl.pallas_call(
        functools.partial(owner_kernel, devices),
        out_shape=[jax.ShapeDtypeStruct((width, states), BF16), jax.ShapeDtypeStruct((count, length, states), F32)]
        + [jax.ShapeDtypeStruct((count, length, states), BF16)] * 3,
        in_specs=[SMEM, SMEM] + [VMEM] * 5,
        out_specs=[VMEM] * 5,
        scratch_shapes=[pltpu.VMEM((width, states), F32), pltpu.VMEM((SPAN, count, length, states), F32)],
        compiler_params=pltpu.CompilerParams(vmem_limit_bytes=24 * 2**20),
        cost_estimate=pl.CostEstimate(flops=2 * 10**9, bytes_accessed=8 * 2**20, transcendentals=0),
        name="owner_state",
    )(rank, resp_prefix, state, *carried)


def sum_kernel(back0, back1, back2, g_keys, g_values, g_tail):
    rows = g_keys.shape[1]
    for half, out in enumerate((g_keys, g_values)):
        total = back0[half]
        for back in (back1, back2):
            total = total + back[half].astype(F32)
        out[0] = total[0:rows]
        for part in range(2):
            lo = half * 1024 + part * 512
            g_tail[:, 0, lo : lo + 512] = total[rows + 8 * part : rows + 8 * part + 3]


def sum_back(backs, tail_shape):
    rows = backs[0].shape[1] - 16
    width = backs[0].shape[2]
    return pl.pallas_call(
        sum_kernel,
        out_shape=[
            jax.ShapeDtypeStruct((1, rows, width), F32),
            jax.ShapeDtypeStruct((1, rows, width), F32),
            jax.ShapeDtypeStruct((tail_shape[1], 1, tail_shape[2]), F32),
        ],
        in_specs=[VMEM] * 3,
        out_specs=[VMEM] * 3,
        name="sum_prefix",
    )(*backs)


def on_device(
    token_inputs,
    state_in,
    state_out,
    log_decay,
    skip_gain,
    conv_weight,
    out_cotangent,
    queries,
    own_keys,
    own_values,
    attn_cotangent,
    resp_length,
    resp_prefix,
    prefix_state,
    prefix_tail,
    prefix_keys,
    prefix_values,
    prefix_length,
):
    devices = lax.axis_size("dp")
    rank = lax.axis_index("dp").astype(jnp.int32).reshape(1)
    count, length, _ = token_inputs.shape
    states = state_out.shape[3]
    write = state_in.reshape(count, length, states)
    read = state_out.reshape(count, length, states)
    state = prefix_state.reshape(-1, states)

    decay = jnp.swapaxes(log_decay, 1, 2)
    packed = pack(prefix_keys, prefix_values, prefix_tail)
    pack_two, pack_last = two_and_last(packed, 1)
    carried = carry(after(resp_length, packed), decay, out_cotangent, read)
    pack_two, pack_last, carried = lax.optimization_barrier((pack_two, pack_last, carried))
    carry_two, carry_last = two_and_last(carried, -1)
    packs = [packed, pack_two, swap(pack_two, 1), pack_last]
    g_inputs, g_tail, conv, g_read = mamba(
        rank, resp_prefix, resp_length, skip_gain, token_inputs, packs, conv_weight, write, read, decay, out_cotangent, devices
    )
    steps = [by for by in (2, 1, 4, 8) if by < devices]
    while 2 * max(steps) < devices:
        steps.append(2 * max(steps))
    whole = devices & (devices - 1) == 0
    swaps = iter(steps if whole else [])

    def next_step():
        by = next(swaps, None)
        return jnp.zeros_like(conv) if by is None else swap(conv, by)

    moved = next_step()
    g_queries, *backs = attention(
        rank, resp_prefix, resp_length, prefix_length, queries, attn_cotangent, own_keys, own_values, packs, g_tail, devices
    )
    *backs, moved, carry_two = lax.optimization_barrier((*backs, moved, carry_two))
    conv = conv + moved
    own, two, last, other = backs
    other = swap(other, 1)
    last = lax.ppermute(last, "dp", behind(devices))
    carry_relay = swap(carry_two, 1)
    moved = next_step()
    two = (two.astype(F32) + other.astype(F32)).astype(BF16)
    chosen = after(resp_prefix, two, moved)
    two = shift(two, -2)
    g_state, *reads = owner(rank, chosen, state, [carried, carry_two, carry_relay, carry_last], devices)
    reads = [reads[0]] + [shift(reads[by], by) for by in range(1, SPAN)]
    conv = after(conv + moved, *reads[:1])
    moved = next_step()
    own, moved = lax.optimization_barrier((own, moved))
    conv = conv + moved
    moved = next_step()
    sums = sum_back([own, two, last], prefix_tail.shape)
    *sums, moved, r0, r1, r2, r3 = lax.optimization_barrier((*sums, moved, *reads))
    conv = conv + moved
    g_prefix_keys, g_prefix_values, g_prefix_tail = sums
    for by in swaps:
        conv = conv + swap(conv, by)
    if not whole:
        conv = lax.psum(conv, "dp")
    for part in (r0, r1, r2, r3):
        g_read = g_read + part.astype(F32)
    token_total = count * length * devices
    grad_conv = conv * (1.0 / math.sqrt(token_total))
    return (
        g_inputs,
        g_read.astype(BF16).reshape(state_out.shape),
        g_queries,
        g_state.reshape(prefix_state.shape),
        jnp.swapaxes(g_prefix_tail, 0, 1),
        g_prefix_keys,
        g_prefix_values,
        grad_conv,
    )


def solution(mesh):
    split = ("groups", "dp")
    placed = (
        P(split, None, None),
        P(split, None, None, None),
        P(split, None, None, None),
        P(split, None, None),
        P(),
        P(),
        P(split, None, None),
        P(split, None, None),
        P(split, None, None),
        P(split, None, None),
        P(split, None, None),
        P(split),
        P("groups"),
        P(split, None, None, None),
        P(split, None, None),
        P(split, None, None),
        P(split, None, None),
        P("groups"),
    )
    return jax.shard_map(
        on_device,
        mesh=mesh,
        in_specs=placed,
        out_specs=(
            P(split, None, None),
            P(split, None, None, None),
            P(split, None, None),
            P(split, None, None, None),
            P(split, None, None),
            P(split, None, None),
            P(split, None, None),
            P("groups", None),
        ),
        check_vma=False,
    )
```
